32 devices in a mesh: dp: 8 (over z, y), own: 4 (over x, core).
Axes of the slice: x: 2, y: 2, z: 4, core: 2. Of those that a mesh axis runs over, the one named last changes fastest.
Arguments:
- tokens: bfloat16 [1024, 6144], P('dp', 'own'), may hold values from -6 to 6
- expert_ids: int32 [1024, 2], P('dp'), may hold values from 0 to 7, all different within a row; in each aligned block of 128 rows (0 to 127, 128 to 255, ...) at most 40 rows name the same one
- combine_weights: float32 [1024, 2], P('dp'), may hold values from 0.2 to 1
- gate_weight: bfloat16 [2, 6144, 8192], P(None, 'own', 'dp'), may hold values from -0.078125 to 0.078125
- up_weight: bfloat16 [2, 6144, 8192], P(None, 'own', 'dp'), may hold values from -0.078125 to 0.078125
- down_weight: bfloat16 [2, 8192, 6144], P(None, 'dp', 'own'), may hold values from -0.0625 to 0.0625
- out_grad: bfloat16 [1024, 6144], P('dp', 'own'), may hold values from -6 to 6
Outputs:
- mixed: bfloat16 [1024, 6144], P('dp', 'own')
- token_grad: bfloat16 [1024, 6144], P('dp', 'own')
- gate_grad_weight: float32 [2, 6144, 8192], P(None, 'own', 'dp')
- up_grad_weight: float32 [2, 6144, 8192], P(None, 'own', 'dp')
- down_grad_weight: float32 [2, 8192, 6144], P(None, 'dp', 'own')
The draws below stay inside these ranges and needn't reach their ends.
Inputs may be any that keep to these rules, and one draw needn't show every extreme that they name: `expert_ids`: each row names 2 different experts. The 128 rows of one index of dp name each expert at most 40 times, and in every draw some expert is named exactly 40 times by the rows of one index of dp.
All inputs are finite; a program needn't handle non-finite values.
Results may differ from the reference program's by a relative error of at most 0.024.
Values may be sent and summed in bfloat16 or wider, within the bound.
No kernel may reach another device: no remote copies, remote signals or barrier semaphores. Data moves between devices by JAX's collectives and lax.ppermute only.
A program may use at most 192 MiB of HBM per device.

```python
import math
import jax
import jax.numpy as jnp
import numpy as np
from jax import lax

D = 6144
FF = 8192
NEXP = 8
TOPK = 2
E = 2
TOK_DEV = 128
CAP = 40
TOKENS = 1024
N_DP = 8
N_OWN = 4


def level_of(stream_key, dims, cuts, smallest, high):
    def one(dim, blocks):
        heights = jax.random.uniform(jax.random.fold_in(jax.random.fold_in(stream_key, 6), dim), (blocks,), jnp.float32, smallest / len(cuts), high / len(cuts))
        return jnp.repeat(jnp.exp(heights), dims[dim] // blocks).reshape((-1,) + (1,) * (len(dims) - dim - 1))

    factor_of = one(*cuts[0])
    for cut in cuts[1:]:
        factor_of = factor_of * one(*cut)
    return factor_of


def shared_out(own_key, own, number, rows, count, top, bound, slope):
    order = jax.random.permutation(own_key, count)
    heavy_load, common = load_shares(count, rows * top, bound, slope, True), load_shares(count, rows * top, bound, slope, False)
    places = jnp.arange(count)

    def named(sizes, rotation):
        used = int((sizes > 0).sum())
        fixed = max(1, used // 4)
        shifted = fixed + (places - fixed + rotation * (used - fixed)) % max(1, count - fixed)
        return jnp.zeros((count,), jnp.int32).at[order[jnp.where(places < fixed, places, shifted)]].set(jnp.asarray(sizes, jnp.int32))

    sizes = jnp.where(number % 4 == 0, named(heavy_load, number // 4), named(common, number - number // 4 - 1))
    mixed = jax.random.permutation(jax.random.fold_in(own, 3), count)
    donor, sink = mixed[0:count // 2 * 2:2], mixed[1:count // 2 * 2:2]
    slack = jnp.minimum(sizes[donor] - 1, bound - sizes[sink]) // 2
    slack = jnp.where((donor == order[0]) | (sink == order[0]) | (sizes[sink] == 0), 0, jnp.maximum(slack, 0))
    shifted = jax.random.randint(jax.random.fold_in(own, 4), (count // 2,), 0, 1 << 20) % (slack + 1)
    sizes = sizes.at[donor].add(-shifted).at[sink].add(shifted)
    members = jnp.searchsorted(jnp.cumsum(sizes), jnp.arange(rows * top), side="right").astype(jnp.int32)
    listing = members.reshape(top, rows).T
    listing = listing[jax.random.permutation(jax.random.fold_in(own, 1), rows)]
    rotation = jax.random.randint(jax.random.fold_in(own, 2), (rows, 1), 0, top)
    return jnp.take_along_axis(listing, (jnp.arange(top)[None, :] + rotation) % top, axis=1)


def load_shares(count, total, most, skew, full):
    weights = [(1 << 20) // math.isqrt(rank ** skew) + 1 for rank in range(1, count + 1)]
    largest = most if full else min(most, max(-(-total // count), total * weights[0] // sum(weights)))
    least = 1 if total - largest >= count - 1 else 0
    counts, spare = [largest] + [least] * (count - 1), total - largest - least * (count - 1)
    while spare > 0:
        candidates = [i for i in range(1, count) if counts[i] < largest] or [i for i in range(1, count) if counts[i] < most]
        whole, budget = sum([weights[i] for i in candidates]), spare
        for i in candidates:
            more = min(most - counts[i], max(1, budget * weights[i] // whole), spare)
            counts[i] = counts[i] + more
            spare = spare - more
    return np.array(counts)


def gaussian(rng, dims, scale, reach, cuts=(), held_as=jnp.bfloat16):
    gain = level_of(rng, dims, cuts, -0.22, 0.18) if cuts else 1.0
    values = jax.random.normal(rng, dims, jnp.float32) * scale * gain
    return jnp.minimum(jnp.maximum(values, -reach), reach).astype(held_as)


def setup_inputs(seed: int = 0) -> dict:
    seeds = jax.random.split(jax.random.key(seed), 8)
    tokens = gaussian(seeds[0], (TOKENS, D), 1.0, 6.0, ((0, 8), (1, 4)))
    expert_ids_keys = jax.random.split(jax.random.fold_in(seeds[1], 1), TOKENS // TOK_DEV)
    expert_ids_turns = jax.random.permutation(jax.random.fold_in(seeds[1], 3), TOKENS // TOK_DEV)
    expert_ids = jax.vmap(lambda own, number: shared_out(jax.random.fold_in(seeds[1], 2), own, number, TOK_DEV, NEXP, TOPK, CAP, 1))(expert_ids_keys, expert_ids_turns).reshape((TOKENS, TOPK))
    combine_weights = jnp.clip(0.2 + 0.8 * jax.random.uniform(seeds[2], (TOKENS, TOPK), jnp.float32) ** level_of(seeds[2], (TOKENS, TOPK), ((0, 8),), -0.2, 0.2), 0.2, 1.0)
    gate_weight = gaussian(seeds[3], (E, D, FF), D ** -0.5, 0.078125, ((1, 4), (2, 8)))
    up_weight = gaussian(seeds[4], (E, D, FF), D ** -0.5, 0.078125, ((1, 4), (2, 8)))
    down_weight = gaussian(seeds[5], (E, FF, D), FF ** -0.5, 0.0625, ((1, 8), (2, 4)))
    out_grad = gaussian(seeds[6], (TOKENS, D), 1.0, 6.0, ((0, 8), (1, 4)))
    return dict(tokens=tokens, expert_ids=expert_ids, combine_weights=combine_weights, gate_weight=gate_weight, up_weight=up_weight, down_weight=down_weight, out_grad=out_grad)


def slot_order(shard_ids, expert):
    chosen = shard_ids == expert
    routed = jnp.any(chosen, axis=-1)
    position = (jnp.cumsum(routed.astype(jnp.int32)) - 1).astype(jnp.int32)
    slot_ids = jnp.arange(CAP, dtype=jnp.int32)
    matches = routed[None, :] & (position[None, :] == slot_ids[:, None])
    token_ids = jnp.arange(shard_ids.shape[0], dtype=jnp.int32)
    source = jnp.sum(jnp.where(matches, token_ids[None, :], 0), axis=1).astype(jnp.int32)
    filled = jnp.any(matches, axis=1)
    target = jnp.where(routed, position, 0).astype(jnp.int32)
    return chosen, routed, source, filled, target


def tables_for(expert_ids, combine_weights, expert):
    shards = expert_ids.reshape(N_DP, TOK_DEV, TOPK)

    def one_shard(shard_ids):
        return slot_order(shard_ids, expert)

    chosen, routed, source, filled, target = jax.vmap(one_shard)(shards)
    shard_base = jnp.arange(N_DP, dtype=jnp.int32)
    source = (source + shard_base[:, None] * TOK_DEV).astype(jnp.int32).reshape(-1)
    target = (target + shard_base[:, None] * CAP).astype(jnp.int32).reshape(-1)
    weight = jnp.sum(jnp.where(chosen.reshape(-1, TOPK), combine_weights, 0.0), axis=-1)
    return routed.reshape(-1), source, filled.reshape(-1), target, weight


def own_blocks(left, right):
    row_total = left.shape[0]
    left_blocks = left.astype(jnp.float32).reshape(row_total, N_OWN, D // N_OWN)
    right_blocks = right.astype(jnp.float32).reshape(N_OWN, D // N_OWN, right.shape[1])
    partial_sums = jnp.einsum("rjd,jdf->jrf", left_blocks, right_blocks).astype(jnp.bfloat16)
    partial_sums = lax.optimization_barrier(partial_sums)
    return jnp.sum(partial_sums.astype(jnp.float32), axis=0)


def dp_blocks(lefts, rights):
    row_total = lefts[0].shape[0]
    width = rights[0].shape[1]
    left_blocks = tuple(item.reshape(row_total, N_DP, FF // N_DP).transpose(1, 0, 2) for item in lefts)
    right_blocks = tuple(item.reshape(N_DP, FF // N_DP, width) for item in rights)

    def step(carry, pieces):
        left_pieces, right_pieces = pieces
        block_sum = jnp.zeros((row_total, width), jnp.float32)
        for left_item, right_item in zip(left_pieces, right_pieces):
            block_sum = block_sum + jnp.dot(left_item, right_item, preferred_element_type=jnp.float32)
        rounded = lax.optimization_barrier(block_sum.astype(jnp.bfloat16))
        return carry + rounded.astype(jnp.float32), None

    result, unused = lax.scan(step, jnp.zeros((row_total, width), jnp.float32), (left_blocks, right_blocks))
    return result


def reference(tokens, expert_ids, combine_weights, gate_weight, up_weight, down_weight, out_grad):
    mixed = jnp.zeros((TOKENS, D), jnp.float32)
    token_grad = jnp.zeros((TOKENS, D), jnp.float32)
    gate_grads = []
    up_grads = []
    down_grads = []
    for expert in range(E):
        routed, source, filled, target, weight = tables_for(expert_ids, combine_weights, expert)
        dispatched = jnp.where(filled[:, None], tokens[source], 0).astype(jnp.bfloat16)
        gate_sum = own_blocks(dispatched, gate_weight[expert])
        up_sum = own_blocks(dispatched, up_weight[expert])
        sigma = jax.nn.sigmoid(gate_sum)
        swish = gate_sum * sigma
        hidden = (swish * up_sum).astype(jnp.bfloat16)
        expert_out = dp_blocks((hidden,), (down_weight[expert],))
        token_weight = jnp.where(routed, weight, 0.0)
        mixed = mixed + token_weight[:, None] * expert_out[target]
        slot_weight = jnp.where(filled, weight[source], 0.0)
        scaled = (slot_weight[:, None] * out_grad[source].astype(jnp.float32)).astype(jnp.bfloat16)
        hidden_grad = own_blocks(scaled, down_weight[expert].T)
        gate_grad = (hidden_grad * up_sum * sigma * (1.0 + gate_sum * (1.0 - sigma))).astype(jnp.bfloat16)
        up_grad = (hidden_grad * swish).astype(jnp.bfloat16)
        row_grad = dp_blocks((gate_grad, up_grad), (gate_weight[expert].T, up_weight[expert].T))
        token_grad = token_grad + jnp.where(routed[:, None], row_grad[target], 0.0)
        gate_grads.append(jnp.dot(dispatched.T, gate_grad, preferred_element_type=jnp.float32))
        up_grads.append(jnp.dot(dispatched.T, up_grad, preferred_element_type=jnp.float32))
        down_grads.append(jnp.dot(hidden.T, scaled, preferred_element_type=jnp.float32))
    return (mixed.astype(jnp.bfloat16), token_grad.astype(jnp.bfloat16),
            jnp.stack(gate_grads), jnp.stack(up_grads), jnp.stack(down_grads))
```

```python
import functools
import jax
import jax.numpy as jnp
from jax import lax
from jax.experimental import pallas as pl
from jax.experimental.pallas import tpu as pltpu
from jax.sharding import PartitionSpec as P

CAP = 40
BF = jnp.bfloat16
F32 = jnp.float32
MIB = 1024 * 1024
ROWS = (((0,), (0,)), ((), ()))
LAST = (((1,), (1,)), ((), ()))


def shape(dims, dtype=BF):
    return jax.ShapeDtypeStruct(dims, dtype)


def whole(dims):
    return pl.BlockSpec(dims, lambda *a: (0,) * len(dims))


def cost(flops, size):
    return pl.CostEstimate(flops=int(flops), bytes_accessed=int(size), transcendentals=0)


def mm(a, b):
    return jnp.dot(a, b, preferred_element_type=F32)


def dispatch_kernel(experts, ids, cw, tokens, grad, *outs):
    rows, scaled, pick, weight = outs[:experts], outs[experts : 2 * experts], outs[-2], outs[-1]
    n = ids.shape[0]
    tri = (
        lax.broadcasted_iota(jnp.int32, (n, n), 0) >= lax.broadcasted_iota(jnp.int32, (n, n), 1)
    ).astype(BF)
    slots = lax.broadcasted_iota(jnp.int32, (n, CAP), 1)
    token = tokens[...]
    cot = grad[...].astype(F32)
    for e in range(experts):
        chosen = ids[...] == e
        routed = jnp.sum(chosen.astype(F32), axis=1, keepdims=True)
        w = jnp.sum(jnp.where(chosen, cw[...], 0.0), axis=1, keepdims=True)
        position = mm(tri, jnp.broadcast_to(routed, (n, 128)).astype(BF))[:, :CAP]
        match = (position.astype(jnp.int32) - 1 == slots) & (routed > 0.0)
        match = jnp.where(match, 1.0, 0.0).astype(BF)
        pick[e] = match
        weight[e] = jnp.broadcast_to(w, (n, 128))
        rows[e][...] = lax.dot_general(match, token, ROWS, preferred_element_type=F32).astype(BF)
        scaled[e][...] = lax.dot_general(
            match, (w * cot).astype(BF), ROWS, preferred_element_type=F32
        ).astype(BF)


def dispatch(ids, cw, tokens, grad, experts):
    n, d = tokens.shape
    outs = [shape((CAP, d))] * (2 * experts) + [
        shape((experts, n, CAP)),
        shape((experts, n, 128), F32),
    ]
    res = pl.pallas_call(
        functools.partial(dispatch_kernel, experts),
        out_shape=outs,
        compiler_params=pltpu.CompilerParams(vmem_limit_bytes=16 * MIB),
        cost_estimate=cost(4 * experts * CAP * n * d, 8 * n * d),
        name="dispatch",
    )(ids, cw, tokens, grad)
    return res[:experts], res[experts : 2 * experts], res[-2], res[-1]


def project_kernel(parts, transposed, core, first, second, *refs):
    weights, keep, send = refs[:parts], refs[parts], refs[parts + 1]
    j, half = pl.program_id(0), pl.num_programs(0) // 2
    h = first.shape[0]

    def store(out):
        for p in range(parts):
            w = weights[p][0]
            for i, ref in enumerate((first, second)):
                if transposed:
                    val = lax.dot_general(ref[...], w, LAST, preferred_element_type=F32)
                else:
                    val = mm(ref[...], w)
                out[p, i * h : (i + 1) * h, :] = val.astype(BF)

    @pl.when(j < half)
    def _():
        store(keep)

    @pl.when(j >= half)
    def _():
        store(send)


def project(core, first, second, weights, expert, transposed):
    h, d = first.shape
    f = weights[0].shape[1] if transposed else weights[0].shape[2]
    fb = min(256, f // 2)
    n = f // fb
    parts = len(weights)

    def block(j, c):
        return (j + c[0] * (n // 2)) % n

    if transposed:
        wspec = pl.BlockSpec((1, fb, d), lambda j, c: (expert, block(j, c), 0))
    else:
        wspec = pl.BlockSpec((1, d, fb), lambda j, c: (expert, 0, block(j, c)))
    grid_spec = pltpu.PrefetchScalarGridSpec(
        num_scalar_prefetch=1,
        grid=(n,),
        in_specs=[whole((h, d)), whole((h, d))] + [wspec] * parts,
        out_specs=[
            pl.BlockSpec((parts, 2 * h, fb), lambda j, c: (0, 0, jnp.minimum(j, n // 2 - 1))),
            pl.BlockSpec((parts, 2 * h, fb), lambda j, c: (0, 0, jnp.maximum(j - n // 2, 0))),
        ],
    )
    return pl.pallas_call(
        functools.partial(project_kernel, parts, transposed),
        grid_spec=grid_spec,
        out_shape=[shape((parts, 2 * h, f // 2))] * 2,
        compiler_params=pltpu.CompilerParams(vmem_limit_bytes=24 * MIB),
        cost_estimate=cost(4 * h * d * f * parts, 2 * d * f * parts + 4 * h * d),
        name="hidden_grad_part" if transposed else "gate_up_part",
    )(core, first, second, *weights)


def back_kernel(parts, transposed, core, *refs):
    acts, weights, keep, send = (
        refs[: 2 * parts],
        refs[2 * parts : 4 * parts],
        refs[4 * parts],
        refs[4 * parts + 1],
    )
    total = None
    for a, w in zip(acts, weights):
        if transposed:
            val = lax.dot_general(a[...], w[0], LAST, preferred_element_type=F32)
        else:
            val = mm(a[...], w[0])
        total = val if total is None else total + val
    h = keep.shape[0]
    keep[...] = total[:h].astype(BF)
    send[...] = total[h:].astype(BF)


def back(core, acts, weights, expert, transposed):
    r, half = acts[0].shape
    d = weights[0].shape[1] if transposed else weights[0].shape[2]
    db = 256 if d % 256 == 0 else 128
    parts = len(weights)
    wspecs, warrs = [], []
    for p in range(parts):
        for b in range(2):
            if transposed:
                wspecs.append(
                    pl.BlockSpec((1, db, half), lambda j, c, b=b: (expert, j, (c[0] + b) % 2))
                )
            else:
                wspecs.append(
                    pl.BlockSpec((1, half, db), lambda j, c, b=b: (expert, (c[0] + b) % 2, j))
                )
            warrs.append(weights[p])
    grid_spec = pltpu.PrefetchScalarGridSpec(
        num_scalar_prefetch=1,
        grid=(d // db,),
        in_specs=[whole((r, half))] * (2 * parts) + wspecs,
        out_specs=[pl.BlockSpec((r // 2, db), lambda j, c: (0, j))] * 2,
    )
    return pl.pallas_call(
        functools.partial(back_kernel, parts, transposed),
        grid_spec=grid_spec,
        out_shape=[shape((r // 2, d))] * 2,
        compiler_params=pltpu.CompilerParams(vmem_limit_bytes=24 * MIB),
        cost_estimate=cost(4 * r * d * half * parts, 4 * d * half * parts + 2 * r * d),
        name="row_grad_part" if transposed else "expert_part",
    )(core, *acts, *warrs)


def add_kernel(keep, got, out):
    out[...] = (keep[...].astype(F32) + got[...].astype(F32)).astype(BF)


def add(keep, got):
    return pl.pallas_call(
        add_kernel,
        out_shape=shape(keep.shape),
        compiler_params=pltpu.CompilerParams(vmem_limit_bytes=16 * MIB),
        cost_estimate=cost(keep.size, 6 * keep.size),
        name="add",
    )(keep, got)


def halve_kernel(keep, got, out_keep, out_send):
    h = out_keep.shape[0]
    total = (keep[...].astype(F32) + got[...].astype(F32)).astype(BF)
    out_keep[...] = total[:h]
    out_send[...] = total[h:]


def halve(keep, got):
    r, d = keep.shape
    return pl.pallas_call(
        halve_kernel,
        out_shape=[shape((r // 2, d))] * 2,
        compiler_params=pltpu.CompilerParams(vmem_limit_bytes=16 * MIB),
        cost_estimate=cost(keep.size, 6 * keep.size),
        name="halve",
    )(keep, got)


def join_kernel(a, b, out):
    n = a.shape[0]
    out[:n] = a[...]
    out[n:] = b[...]


def join(a, b):
    return jnp.concatenate([a, b], axis=0)


def hidden_kernel(n, keep, got, *refs):
    others, sums, hidden = refs[:n], refs[n], refs[n + 1]
    total = keep[...].astype(F32) + got[...].astype(F32)
    for ref in others:
        total = total + ref[...].astype(F32)
    sums[...] = total
    gate, up = total[0], total[1]
    hidden[...] = (gate * jax.nn.sigmoid(gate) * up).astype(BF)


def hidden_of(keep, got, others):
    _, r, half = keep.shape
    blk = min(r, 320)
    spec = pl.BlockSpec((2, blk, half), lambda i: (0, i, 0))
    return pl.pallas_call(
        functools.partial(hidden_kernel, len(others)),
        grid=(r // blk,),
        in_specs=[spec] * (2 + len(others)),
        out_specs=[spec, pl.BlockSpec((blk, half), lambda i: (i, 0))],
        out_shape=[shape((2, r, half), F32), shape((r, half))],
        compiler_params=pltpu.CompilerParams(vmem_limit_bytes=24 * MIB),
        cost_estimate=cost(20 * r * half, 20 * r * half),
        name="hidden",
    )(keep, got, *others)


def grads_kernel(n, sums, keep, got, *refs):
    others, out = refs[:n], refs[n]
    total = keep[0].astype(F32) + got[0].astype(F32)
    for ref in others:
        total = total + ref[0].astype(F32)
    gate, up = sums[0], sums[1]
    sig = jax.nn.sigmoid(gate)
    out[0] = (total * up * sig * (1.0 + gate * (1.0 - sig))).astype(BF)
    out[1] = (total * gate * sig).astype(BF)


def grads_of(sums, keep, got, others):
    _, r, half = sums.shape
    blk = min(r, 320)
    one = pl.BlockSpec((1, blk, half), lambda i: (0, i, 0))
    two = pl.BlockSpec((2, blk, half), lambda i: (0, i, 0))
    return pl.pallas_call(
        functools.partial(grads_kernel, len(others)),
        grid=(r // blk,),
        in_specs=[two] + [one] * (2 + len(others)),
        out_specs=two,
        out_shape=shape((2, r, half)),
        compiler_params=pltpu.CompilerParams(vmem_limit_bytes=24 * MIB),
        cost_estimate=cost(20 * r * half, 20 * r * half),
        name="gate_up_grads",
    )(sums, keep, got, *others)


def weight_kernel(pairs, has_prev, by_columns, core, *refs):
    refs = list(refs)
    first, second = refs[0], refs[1]
    acts = refs[2 : 2 + 2 * pairs]
    outs = refs[len(refs) - pairs :]
    b = pl.program_id(0)
    h = first.shape[0]
    for p in range(pairs):
        for i in range(2):

            @pl.when(b == i)
            def _():
                act = acts[2 * p + i]
                if by_columns:
                    val = lax.dot_general(first[...], act[:h], ROWS, preferred_element_type=F32)
                    val += lax.dot_general(second[...], act[h:], ROWS, preferred_element_type=F32)
                else:
                    val = lax.dot_general(act[:h], first[...], ROWS, preferred_element_type=F32)
                    val += lax.dot_general(act[h:], second[...], ROWS, preferred_element_type=F32)
                outs[p][0] = val


def weight_grads(core, first, second, acts, expert, experts, prev, by_columns):
    h, d = first.shape
    r, half = acts[0].shape
    pairs = len(acts) // 2
    db = 512 if d % 512 == 0 else 128
    n = d // db
    if by_columns:
        out = shape((experts, d, 2 * half), F32)
        ospec = pl.BlockSpec((1, db, half), lambda b, j, c: (expert, j, (c[0] + b) % 2))
    else:
        out = shape((experts, 2 * half, d), F32)
        ospec = pl.BlockSpec((1, half, db), lambda b, j, c: (expert, (c[0] + b) % 2, j))
    rspec = pl.BlockSpec((h, db), lambda b, j, c: (0, j))
    aspecs = [whole((r, half))] * (2 * pairs)
    extra = [] if prev is None else list(prev)
    grid_spec = pltpu.PrefetchScalarGridSpec(
        num_scalar_prefetch=1,
        grid=(2, n),
        in_specs=[rspec, rspec] + aspecs + [pl.BlockSpec(memory_space=pl.ANY)] * len(extra),
        out_specs=[ospec] * pairs,
    )
    aliases = {3 + 2 * pairs + p: p for p in range(len(extra))}
    return pl.pallas_call(
        functools.partial(weight_kernel, pairs, bool(extra), by_columns),
        grid_spec=grid_spec,
        out_shape=[out] * pairs,
        input_output_aliases=aliases,
        compiler_params=pltpu.CompilerParams(vmem_limit_bytes=24 * MIB),
        cost_estimate=cost(4 * r * d * half * pairs, 8 * d * half * pairs),
        name="gate_up_weight_grad" if by_columns else "down_weight_grad",
    )(core, first, second, *acts, *extra)


def combine_kernel(experts, weighted, pick, weight, *refs):
    keeps, gots, out = refs[:experts], refs[experts : 2 * experts], refs[-1]
    total = 0.0
    for e in range(experts):
        val = (keeps[e][...].astype(F32) + gots[e][...].astype(F32)).astype(BF)
        val = mm(pick[e], val)
        if weighted:
            val = weight[e][:, :1] * val
        total = total + val
    out[...] = total.astype(BF)


def combine(pick, weight, keeps, gots, weighted):
    experts, n, _ = pick.shape
    d = keeps[0].shape[1]
    return pl.pallas_call(
        functools.partial(combine_kernel, experts, weighted),
        out_shape=shape((n, d)),
        compiler_params=pltpu.CompilerParams(vmem_limit_bytes=16 * MIB),
        cost_estimate=cost(4 * n * CAP * d, 4 * n * d),
        name="combine",
    )(pick, weight, *keeps, *gots)


def build(n_dp, n_own):
    bits = n_dp.bit_length() - 1
    far_first = list(range(bits - 1, -1, -1))

    def swap(x, bit):
        return lax.ppermute(x, "dp", [(i, i ^ (1 << bit)) for i in range(n_dp)])

    def swap_core(x):
        return lax.ppermute(x, "own", [(i, i ^ 1) for i in range(n_own)])

    def shift_x(x):
        return [
            lax.ppermute(x, "own", [(i, (i + 2 * k) % n_own) for i in range(n_own)])
            for k in range(1, n_own // 2)
        ]

    def gather(x):
        for bit in far_first[:-1]:
            x = join(x, swap(x, bit))
        return x, swap(x, far_first[-1])

    def scatter(keep, send):
        for bit in far_first[:0:-1]:
            keep, send = halve(keep, swap(send, bit))
        return keep, swap(send, far_first[0])

    def local(tokens, expert_ids, combine_weights, gate_weight, up_weight, down_weight, out_grad):
        experts = gate_weight.shape[0]
        core = (lax.axis_index("own") % 2).astype(jnp.int32).reshape(1)
        rows, scaled, pick, weight = dispatch(
            expert_ids, combine_weights, tokens, out_grad, experts
        )
        rows = [gather(x) for x in rows]
        scaled = [gather(x) for x in scaled]
        sums, hiddens, outs = [], [], []
        for e in range(experts):
            keep, send = project(core, *rows[e], [gate_weight, up_weight], e, False)
            got = swap_core(send)
            total, mine = hidden_of(keep, got, shift_x(add(keep, got)))
            sums.append(total)
            hiddens.append((mine, swap_core(mine)))
            outs.append(scatter(*back(core, hiddens[e], [down_weight], e, False)))
        down_grad = None
        gate_up = None
        row_outs = []
        for e in range(experts):
            keep, send = project(core, *scaled[e], [down_weight], e, True)
            got = swap_core(send)
            mine = grads_of(sums[e], keep, got, shift_x(add(keep, got)))
            other = swap_core(mine)
            acts = (mine[0], other[0], mine[1], other[1])
            row_outs.append(scatter(*back(core, acts, [gate_weight, up_weight], e, True)))
            down_grad = weight_grads(
                core, *scaled[e], hiddens[e], e, experts, down_grad, False
            )
            gate_up = weight_grads(core, *rows[e], acts, e, experts, gate_up, True)
        mixed = combine(pick, weight, [o[0] for o in outs], [o[1] for o in outs], True)
        token_grad = combine(
            pick, weight, [o[0] for o in row_outs], [o[1] for o in row_outs], False
        )
        return mixed, token_grad, gate_up[0], gate_up[1], down_grad[0]

    return local


def solution(mesh):
    local = build(mesh.shape["dp"], mesh.shape["own"])
    in_specs = (
        P("dp", "own"),
        P("dp", None),
        P("dp", None),
        P(None, "own", "dp"),
        P(None, "own", "dp"),
        P(None, "dp", "own"),
        P("dp", "own"),
    )
    out_specs = (
        P("dp", "own"),
        P("dp", "own"),
        P(None, "own", "dp"),
        P(None, "own", "dp"),
        P(None, "dp", "own"),
    )
    return jax.shard_map(local, mesh=mesh, in_specs=in_specs, out_specs=out_specs, check_vma=False)
```

```python
import functools
import jax
import jax.numpy as jnp
from jax import lax
from jax.experimental import pallas as pl
from jax.experimental.pallas import tpu as pltpu
from jax.sharding import PartitionSpec as P

CAP = 40
BF = jnp.bfloat16
F32 = jnp.float32
MIB = 1024 * 1024
LIMIT = 16
VM = pl.BlockSpec(memory_space=pltpu.VMEM)
SM = pl.BlockSpec(memory_space=pltpu.SMEM)
AN = pl.BlockSpec(memory_space=pl.ANY)
ROWS = (((0,), (0,)), ((), ()))
LAST = (((1,), (1,)), ((), ()))


def shape(dims, dtype=BF):
    return jax.ShapeDtypeStruct(dims, dtype)


def mm(a, b):
    return jnp.dot(a, b, preferred_element_type=F32)


class Sequence:
    def __init__(self):
        self.last = None

    def __call__(self, kernel, *args, out_shape, name, in_specs=None, out_specs=None, scratch=(), aliases=None):
        n_in = len(args)
        in_specs = list(in_specs or [VM] * n_in)
        args = list(args)
        extra = 0
        if self.last is not None:
            args.append(self.last)
            in_specs.append(AN)
            extra = 1

        def body(*refs):
            kernel(*refs[:n_in], *refs[n_in + extra :])

        if out_specs is None:
            out_specs = jax.tree.map(lambda o: VM, out_shape)
        out = pl.pallas_call(
            body,
            in_specs=in_specs,
            out_specs=out_specs,
            out_shape=out_shape,
            scratch_shapes=list(scratch),
            input_output_aliases=aliases or {},
            compiler_params=pltpu.CompilerParams(vmem_limit_bytes=LIMIT * MIB),
            cost_estimate=pl.CostEstimate(flops=10**10, bytes_accessed=10**8, transcendentals=0),
            name=name,
        )(*args)
        self.last = min(jax.tree.leaves(out), key=lambda o: o.size)
        return out


def match_of(ids, expert):
    n = ids.shape[1]
    chosen = ids[...] == expert
    routed = jnp.sum(chosen.astype(F32), axis=0, keepdims=True)
    tri = (
        lax.broadcasted_iota(jnp.int32, (n, n), 0) <= lax.broadcasted_iota(jnp.int32, (n, n), 1)
    ).astype(BF)
    position = mm(jnp.broadcast_to(routed, (16, n)).astype(BF), tri)[:1].astype(jnp.int32) - 1
    slots = lax.broadcasted_iota(jnp.int32, (CAP, n), 0)
    match = (position == slots) & (routed > 0.0)
    return chosen, jnp.where(match, 1.0, 0.0)


def rows_kernel(experts, ids, tokens, *outs):
    for e in range(experts):
        _, match = match_of(ids, e)
        outs[e][...] = mm(match.astype(BF), tokens[...]).astype(BF)


def rows_of(run, ids, tokens, experts):
    n, d = tokens.shape
    return run(
        functools.partial(rows_kernel, experts),
        ids,
        tokens,
        out_shape=[shape((CAP, d))] * experts,
        name="rows",
    )


def scaled_kernel(expert, ids, cw, grad, scaled, pick, weight):
    chosen, match = match_of(ids, expert)
    w = jnp.sum(jnp.where(chosen, cw[...], 0.0), axis=0, keepdims=True)
    slot = jnp.sum(match * w, axis=1, keepdims=True)
    scaled[...] = (slot * mm(match.astype(BF), grad[...])).astype(BF)
    pick[...] = match.astype(BF)
    weight[...] = jnp.broadcast_to(slot, weight.shape)


def scaled_of(run, ids, cw, grad, expert):
    n, d = grad.shape
    return run(
        functools.partial(scaled_kernel, expert),
        ids,
        cw,
        grad,
        out_shape=[shape((CAP, d)), shape((CAP, n)), shape((CAP, 128), F32)],
        name="scaled",
    )


def swapped(q):
    n = q.shape[0] // 4
    return jnp.concatenate([q[:n], q[2 * n : 3 * n], q[n : 2 * n], q[3 * n :]], axis=0)


def project_kernel(count, parts, expert, transposed, swap, core, *refs):
    acts, weights = refs[:count], refs[count : count + parts]
    outs = refs[count + parts :]
    act = acts[0][...] if count == 1 else jnp.concatenate([a[...] for a in acts], axis=0)
    if swap:
        act = swapped(act)
    half = outs[0].shape[2]
    fb = min(256, half)
    mine = core[0] * half
    for out, base in zip(outs, (mine, half - mine)):
        for p in range(parts):
            for j in range(half // fb):
                part = pl.ds(pl.multiple_of(base + j * fb, fb), fb)
                if transposed:
                    val = lax.dot_general(
                        act, weights[p][expert, part, :], LAST, preferred_element_type=F32
                    )
                else:
                    val = mm(act, weights[p][expert, :, part])
                out[p, :, j * fb : (j + 1) * fb] = val.astype(BF)


def project(run, core, acts, weights, expert, transposed, swap=False):
    h, d = acts[0].shape
    r = h * len(acts)
    f = weights[0].shape[1] if transposed else weights[0].shape[2]
    parts = len(weights)
    return run(
        functools.partial(project_kernel, len(acts), parts, expert, transposed, swap),
        core,
        *acts,
        *weights,
        in_specs=[SM] + [VM] * (len(acts) + parts),
        out_shape=[shape((parts, r, f // 2))] * 2,
        name="hidden_grad_part" if transposed else "gate_up_part",
    )


def back_kernel(parts, expert, transposed, swap, core, mine, other, *refs):
    weights, keep, send = refs[:parts], refs[parts], refs[parts + 1]
    h, d = keep.shape
    half = mine.shape[2]
    db = 256 if d % 256 == 0 else 128
    first = core[0] * half
    bases = [pl.ds(pl.multiple_of(b, half), half) for b in (first, half - first)]
    for j in range(d // db):
        cols = slice(j * db, (j + 1) * db)
        total = None
        for p in range(parts):
            for act, base in zip((mine, other), bases):
                if transposed:
                    val = lax.dot_general(
                        act[p], weights[p][expert, cols, base], LAST, preferred_element_type=F32
                    )
                else:
                    val = mm(act[p], weights[p][expert, base, cols])
                total = val if total is None else total + val
        total = total.astype(BF)
        if swap:
            total = swapped(total)
        keep[:, cols] = total[:h]
        send[:, cols] = total[h:]


def back(run, core, mine, other, weights, expert, transposed, swap=False):
    parts, r, _ = mine.shape
    d = weights[0].shape[1] if transposed else weights[0].shape[2]
    return run(
        functools.partial(back_kernel, parts, expert, transposed, swap),
        core,
        mine,
        other,
        *weights,
        in_specs=[SM] + [VM] * (2 + parts),
        out_shape=[shape((r // 2, d))] * 2,
        name="row_grad_part" if transposed else "expert_part",
    )


def add_kernel(keep, got, out):
    out[...] = (keep[...].astype(F32) + got[...].astype(F32)).astype(BF)


def add(run, keep, got):
    return run(
        add_kernel,
        keep,
        got,
        out_shape=shape(keep.shape),
        name="add",
    )


def halve_kernel(keep, got, out_keep, out_send):
    h = out_keep.shape[0]
    total = (keep[...].astype(F32) + got[...].astype(F32)).astype(BF)
    out_keep[...] = total[:h]
    out_send[...] = total[h:]


def halve(run, keep, got):
    r, d = keep.shape
    return run(
        halve_kernel,
        keep,
        got,
        out_shape=[shape((r // 2, d))] * 2,
        name="halve",
    )


def join_kernel(a, b, out):
    n = a.shape[0]
    out[:n] = a[...]
    out[n:] = b[...]


def join(run, a, b):
    return run(
        join_kernel,
        a,
        b,
        out_shape=shape((2 * a.shape[0], a.shape[1])),
        name="join",
    )


def total_of(terms):
    total = 0.0
    for ref in terms:
        total = total + ref[...].astype(F32)
    return total


def sum_kernel(*refs):
    refs[-1][...] = total_of(refs[:-1])


def sum_of(run, terms):
    return run(sum_kernel, *terms, out_shape=shape(terms[0].shape, F32), name="sum")


def hidden_kernel(counts, *refs):
    sums, hidden = refs[-2:]
    h = sums.shape[1] // len(counts)
    at = 0
    for i, n in enumerate(counts):
        total = total_of(refs[at : at + n])
        at += n
        sums[:, i * h : (i + 1) * h, :] = total
        gate, up = total[0], total[1]
        hidden[0, i * h : (i + 1) * h, :] = (gate * jax.nn.sigmoid(gate) * up).astype(BF)


def hidden_of(run, groups):
    flat = [t for group in groups for t in group]
    _, h, half = flat[0].shape
    r = h * len(groups)
    return run(
        functools.partial(hidden_kernel, [len(g) for g in groups]),
        *flat,
        out_shape=[shape((2, r, half), F32), shape((1, r, half))],
        name="hidden",
    )


def grads_kernel(sums, *refs):
    terms, out = refs[:-1], refs[-1]
    total = 0.0
    for ref in terms:
        total = total + ref[0].astype(F32)
    gate, up = sums[0], sums[1]
    sig = jax.nn.sigmoid(gate)
    out[0] = (total * up * sig * (1.0 + gate * (1.0 - sig))).astype(BF)
    out[1] = (total * gate * sig).astype(BF)


def grads_of(run, sums, terms):
    _, r, half = sums.shape
    return run(
        grads_kernel,
        sums,
        *terms,
        out_shape=shape((2, r, half)),
        name="gate_up_grads",
    )


SLOTS = 4


def weight_kernel(which, expert, by_columns, swap, core, first, second, mine, other, *refs):
    token, slots, sem = refs[-3:]
    out = refs[-4]
    d = first.shape[1]
    half = mine.shape[2]
    db = slots.shape[1] if by_columns else slots.shape[2]
    token[...] = jnp.zeros(token.shape, F32)
    act = jnp.concatenate([first[...], second[...]], axis=0)
    if swap:
        act = swapped(act)
    base = core[0] * half
    bases = [pl.ds(pl.multiple_of(b, half), half) for b in (base, half - base)]
    pending = []

    def put(val, dst):
        i = len(pending)
        if i >= SLOTS:
            pending[i - SLOTS].wait()
        slots[i % SLOTS] = val
        copy = pltpu.make_async_copy(slots.at[i % SLOTS], dst, sem.at[i % SLOTS])
        copy.start()
        pending.append(copy)

    if by_columns:
        for j in range(d // db):
            cols = slice(j * db, (j + 1) * db)
            turned = act[:, cols].T
            for grads, part in zip((mine, other), bases):
                put(mm(turned, grads[which]), out.at[expert, pl.ds(j * db, db), part])
    else:
        for grads, part in zip((mine, other), bases):
            turned = grads[which].T
            for j in range(d // db):
                cols = slice(j * db, (j + 1) * db)
                put(mm(turned, act[:, cols]), out.at[expert, part, pl.ds(j * db, db)])
    for copy in pending[-SLOTS:]:
        copy.wait()


def weight_grads(run, core, first, second, mine, other, which, expert, experts, prev, by_columns, swap=False):
    h, d = first.shape
    _, r, half = mine.shape
    db = 512 if d % 512 == 0 else 128
    if by_columns:
        out = shape((experts, d, 2 * half), F32)
        slot = (SLOTS, db, half)
    else:
        out = shape((experts, 2 * half, d), F32)
        slot = (SLOTS, half, db)
    extra = [] if prev is None else [prev]
    return run(
        functools.partial(weight_kernel, which, expert, by_columns, swap),
        core,
        first,
        second,
        mine,
        other,
        *extra,
        in_specs=[SM] + [VM] * 4 + [AN] * len(extra),
        out_specs=[AN, VM],
        out_shape=[out, shape((8, 128), F32)],
        scratch=[pltpu.VMEM(slot, F32), pltpu.SemaphoreType.DMA((SLOTS,))],
        aliases={5: 0} if extra else {},
        name="weight_grad",
    )[0]


def combine_kernel(experts, weighted, *refs):
    picks, weights = refs[:experts], refs[experts : 2 * experts]
    keeps, gots = refs[2 * experts : 3 * experts], refs[3 * experts : 4 * experts]
    out = refs[-1]
    total = 0.0
    for e in range(experts):
        val = keeps[e][...].astype(F32) + gots[e][...].astype(F32)
        if weighted:
            val = weights[e][:, :1] * val
        total = total + lax.dot_general(
            picks[e][...], val.astype(BF), ROWS, preferred_element_type=F32
        )
    out[...] = total.astype(BF)


def combine(run, picks, weights, pairs, weighted):
    experts, (_, n) = len(picks), picks[0].shape
    d = pairs[0][0].shape[1]
    args = [*picks, *weights, *[p[0] for p in pairs], *[p[1] for p in pairs]]
    return run(
        functools.partial(combine_kernel, experts, weighted),
        *args,
        out_shape=shape((n, d)),
        name="combine",
    )


def build(n_dp, n_own):
    bits = n_dp.bit_length() - 1
    plain = list(range(bits - 1, -1, -1))
    mixed_order = plain[:-2] + [0, 1]

    def swap(x, bit):
        return lax.ppermute(x, "dp", [(i, i ^ (1 << bit)) for i in range(n_dp)])

    def swap_core(x):
        return lax.ppermute(x, "own", [(i, i ^ 1) for i in range(n_own)])

    def shift_x(x):
        return [
            lax.ppermute(x, "own", [(i, (i + 2 * k) % n_own) for i in range(n_own)])
            for k in range(1, n_own // 2)
        ]

    def gather(run, x, order):
        for bit in order[:-1]:
            got = swap(x, bit)
            yield None
            x = join(run, x, got)
        yield x, swap(x, order[-1])

    def scatter(run, keep, send, order):
        for bit in order[:0:-1]:
            got = swap(send, bit)
            yield None
            keep, send = halve(run, keep, got)
        yield keep, swap(send, order[0])

    def local(tokens, expert_ids, combine_weights, gate_weight, up_weight, down_weight, out_grad):
        run = Sequence()
        experts = gate_weight.shape[0]
        core = (lax.axis_index("own") % 2).astype(jnp.int32).reshape(1)
        ids, cw = expert_ids.T, combine_weights.T
        near = len(plain) - 1

        def steps(gen, n):
            for _ in range(n):
                res = next(gen)
            return res

        def up_gate_part(rows, e):
            keep, send = project(run, core, rows, [gate_weight, up_weight], e, False)
            return keep, swap_core(send)

        def across(part):
            return (*part, *shift_x(add(run, *part)))

        r0, r1 = rows_of(run, ids, tokens, experts)
        a0, a1 = gather(run, r0, plain), gather(run, r1, mixed_order)
        next(a0)
        next(a1)
        steps(a0, near - 1)
        steps(a1, near - 1)
        s0, pick0, weight0 = scaled_of(run, ids, cw, out_grad, 0)
        g0 = gather(run, s0, plain)
        next(g0)
        rows0 = next(a0)
        p0a = up_gate_part(rows0[:1], 0)
        rows1 = next(a1)
        u0a = across(p0a)
        p1a = up_gate_part(rows1[:1], 1)
        steps(g0, near - 1)
        u1a = across(p1a)
        p0b = up_gate_part(rows0[1:], 0)
        scaled0 = next(g0)
        u0b = across(p0b)
        p1b = up_gate_part(rows1[1:], 1)
        u0a = (sum_of(run, u0a),)
        s1, pick1, weight1 = scaled_of(run, ids, cw, out_grad, 1)
        g1 = gather(run, s1, plain)
        next(g1)
        u1b = across(p1b)
        steps(g1, near - 1)
        u1a = (sum_of(run, u1a),)
        scaled1 = next(g1)
        sums0, hidden0 = hidden_of(run, (u0a, u0b))
        hidden0 = (hidden0, swap_core(hidden0))
        hp0 = project(run, core, scaled0, [down_weight], 0, True)
        hp0 = (hp0[0], swap_core(hp0[1]))
        o0 = scatter(run, *back(run, core, *hidden0, [down_weight], 0, False), plain)
        next(o0)
        h0 = across(hp0)
        sums1, hidden1 = hidden_of(run, (u1a, u1b))
        hidden1 = (hidden1, swap_core(hidden1))
        hp1 = project(run, core, scaled1, [down_weight], 1, True, True)
        hp1 = (hp1[0], swap_core(hp1[1]))
        o1 = scatter(run, *back(run, core, *hidden1, [down_weight], 1, False, True), plain)
        next(o1)
        h1 = across(hp1)
        d0 = grads_of(run, sums0, h0)
        d0 = (d0, swap_core(d0))
        down = weight_grads(run, core, *scaled0, *hidden0, 0, 0, experts, None, False)
        q0 = scatter(run, *back(run, core, *d0, [gate_weight, up_weight], 0, True), plain)
        next(q0)
        next(o0)
        d1 = grads_of(run, sums1, h1)
        d1 = (d1, swap_core(d1))
        down = weight_grads(run, core, *scaled1, *hidden1, 0, 1, experts, down, False, True)
        q1 = scatter(run, *back(run, core, *d1, [gate_weight, up_weight], 1, True), mixed_order)
        next(q1)
        out0 = steps(o0, near - 1)
        next(o1)
        gate = weight_grads(run, core, *rows0, *d0, 0, 0, experts, None, True)
        next(q1)
        next(q0)
        up = weight_grads(run, core, *rows0, *d0, 1, 0, experts, None, True)
        out1 = steps(o1, near - 1)
        row1 = steps(q1, near - 1)
        gate = weight_grads(run, core, *rows1, *d1, 0, 1, experts, gate, True)
        row0 = steps(q0, near - 1)
        up = weight_grads(run, core, *rows1, *d1, 1, 1, experts, up, True)
        picks, weights = (pick0, pick1), (weight0, weight1)
        mixed = combine(run, picks, weights, (out0, out1), True)
        token_grad = combine(run, picks, weights, (row0, row1), False)
        return mixed, token_grad, gate, up, down

    return local


def solution(mesh):
    local = build(mesh.shape["dp"], mesh.shape["own"])
    in_specs = (
        P("dp", "own"),
        P("dp", None),
        P("dp", None),
        P(None, "own", "dp"),
        P(None, "own", "dp"),
        P(None, "dp", "own"),
        P("dp", "own"),
    )
    out_specs = (
        P("dp", "own"),
        P("dp", "own"),
        P(None, "own", "dp"),
        P(None, "own", "dp"),
        P(None, "dp", "own"),
    )
    return jax.shard_map(local, mesh=mesh, in_specs=in_specs, out_specs=out_specs, check_vma=False)
```

```python
import functools
import jax
import jax.numpy as jnp
from jax import lax
from jax.experimental import pallas as pl
from jax.experimental.pallas import tpu as pltpu
from jax.sharding import PartitionSpec as P

CAP = 40
BF = jnp.bfloat16
F32 = jnp.float32
MIB = 1024 * 1024
LIMIT = 16
VM = pl.BlockSpec(memory_space=pltpu.VMEM)
SM = pl.BlockSpec(memory_space=pltpu.SMEM)
AN = pl.BlockSpec(memory_space=pl.ANY)
ROWS = (((0,), (0,)), ((), ()))
LAST = (((1,), (1,)), ((), ()))


def shape(dims, dtype=BF):
    return jax.ShapeDtypeStruct(dims, dtype)


def mm(a, b):
    return jnp.dot(a, b, preferred_element_type=F32)


class Sequence:
    def __init__(self):
        self.last = None

    def __call__(self, kernel, *args, out_shape, name, in_specs=None, out_specs=None, scratch=(), aliases=None):
        n_in = len(args)
        in_specs = list(in_specs or [VM] * n_in)
        args = list(args)
        extra = 0
        if self.last is not None:
            args.append(self.last)
            in_specs.append(AN)
            extra = 1

        def body(*refs):
            kernel(*refs[:n_in], *refs[n_in + extra :])

        if out_specs is None:
            out_specs = jax.tree.map(lambda o: VM, out_shape)
        out = pl.pallas_call(
            body,
            in_specs=in_specs,
            out_specs=out_specs,
            out_shape=out_shape,
            scratch_shapes=list(scratch),
            input_output_aliases=aliases or {},
            compiler_params=pltpu.CompilerParams(vmem_limit_bytes=LIMIT * MIB),
            cost_estimate=pl.CostEstimate(flops=10**10, bytes_accessed=10**8, transcendentals=0),
            name=name,
        )(*args)
        self.last = min(jax.tree.leaves(out), key=lambda o: o.size)
        return out


def match_of(ids, expert):
    n = ids.shape[1]
    chosen = ids[...] == expert
    routed = jnp.sum(chosen.astype(F32), axis=0, keepdims=True)
    tri = (
        lax.broadcasted_iota(jnp.int32, (n, n), 0) <= lax.broadcasted_iota(jnp.int32, (n, n), 1)
    ).astype(BF)
    position = mm(jnp.broadcast_to(routed, (16, n)).astype(BF), tri)[:1].astype(jnp.int32) - 1
    slots = lax.broadcasted_iota(jnp.int32, (CAP, n), 0)
    match = (position == slots) & (routed > 0.0)
    return chosen, jnp.where(match, 1.0, 0.0)


def rows_kernel(expert, ids, tokens, out):
    _, match = match_of(ids, expert)
    out[...] = mm(match.astype(BF), tokens[...]).astype(BF)


def rows_of(run, ids, tokens, expert):
    return run(
        functools.partial(rows_kernel, expert),
        ids,
        tokens,
        out_shape=shape((CAP, tokens.shape[1])),
        name="rows",
    )


def scaled_kernel(expert, ids, cw, grad, scaled, pick, weight):
    chosen, match = match_of(ids, expert)
    w = jnp.sum(jnp.where(chosen, cw[...], 0.0), axis=0, keepdims=True)
    slot = jnp.sum(match * w, axis=1, keepdims=True)
    scaled[...] = (slot * mm(match.astype(BF), grad[...])).astype(BF)
    pick[...] = match.astype(BF)
    weight[...] = jnp.broadcast_to(slot, weight.shape)


def scaled_of(run, ids, cw, grad, expert):
    n, d = grad.shape
    return run(
        functools.partial(scaled_kernel, expert),
        ids,
        cw,
        grad,
        out_shape=[shape((CAP, d)), shape((CAP, n)), shape((CAP, 128), F32)],
        name="scaled",
    )


def tick_kernel(out):
    out[...] = jnp.zeros(out.shape, F32)


def tick(run):
    run(tick_kernel, out_shape=shape((8, 128), F32), name="tick")


def swapped(q):
    n = q.shape[0] // 4
    return jnp.concatenate([q[:n], q[2 * n : 3 * n], q[n : 2 * n], q[3 * n :]], axis=0)


def project_kernel(count, parts, expert, transposed, swap, core, *refs):
    acts, weights = refs[:count], refs[count : count + parts]
    outs = refs[count + parts :]
    act = acts[0][...] if count == 1 else jnp.concatenate([a[...] for a in acts], axis=0)
    if swap:
        act = swapped(act)
    half = outs[0].shape[2]
    fb = min(256, half)
    mine = core[0] * half
    for out, base in zip(outs, (mine, half - mine)):
        for p in range(parts):
            for j in range(half // fb):
                part = pl.ds(pl.multiple_of(base + j * fb, fb), fb)
                if transposed:
                    val = lax.dot_general(
                        act, weights[p][expert, part, :], LAST, preferred_element_type=F32
                    )
                else:
                    val = mm(act, weights[p][expert, :, part])
                out[p, :, j * fb : (j + 1) * fb] = val.astype(BF)


def project(run, core, acts, weights, expert, transposed, swap=False):
    h, d = acts[0].shape
    r = h * len(acts)
    f = weights[0].shape[1] if transposed else weights[0].shape[2]
    parts = len(weights)
    return run(
        functools.partial(project_kernel, len(acts), parts, expert, transposed, swap),
        core,
        *acts,
        *weights,
        in_specs=[SM] + [VM] * (len(acts) + parts),
        out_shape=[shape((parts, r, f // 2))] * 2,
        name="hidden_grad_part" if transposed else "gate_up_part",
    )


def back_kernel(parts, expert, transposed, swap, core, mine, other, *refs):
    weights, keep, send = refs[:parts], refs[parts], refs[parts + 1]
    h, d = keep.shape
    half = mine.shape[2]
    db = 256 if d % 256 == 0 else 128
    first = core[0] * half
    bases = [pl.ds(pl.multiple_of(b, half), half) for b in (first, half - first)]
    for j in range(d // db):
        cols = slice(j * db, (j + 1) * db)
        total = None
        for p in range(parts):
            for act, base in zip((mine, other), bases):
                if transposed:
                    val = lax.dot_general(
                        act[p], weights[p][expert, cols, base], LAST, preferred_element_type=F32
                    )
                else:
                    val = mm(act[p], weights[p][expert, base, cols])
                total = val if total is None else total + val
        total = total.astype(BF)
        if swap:
            total = swapped(total)
        keep[:, cols] = total[:h]
        send[:, cols] = total[h:]


def back(run, core, mine, other, weights, expert, transposed, swap=False):
    parts, r, _ = mine.shape
    d = weights[0].shape[1] if transposed else weights[0].shape[2]
    return run(
        functools.partial(back_kernel, parts, expert, transposed, swap),
        core,
        mine,
        other,
        *weights,
        in_specs=[SM] + [VM] * (2 + parts),
        out_shape=[shape((r // 2, d))] * 2,
        name="row_grad_part" if transposed else "expert_part",
    )


def add_kernel(keep, got, out):
    out[...] = (keep[...].astype(F32) + got[...].astype(F32)).astype(BF)


def add(run, keep, got):
    return run(
        add_kernel,
        keep,
        got,
        out_shape=shape(keep.shape),
        name="add",
    )


def halve_kernel(keep, got, out_keep, out_send):
    h = out_keep.shape[0]
    total = (keep[...].astype(F32) + got[...].astype(F32)).astype(BF)
    out_keep[...] = total[:h]
    out_send[...] = total[h:]


def halve(run, keep, got):
    r, d = keep.shape
    return run(
        halve_kernel,
        keep,
        got,
        out_shape=[shape((r // 2, d))] * 2,
        name="halve",
    )


def join_kernel(a, b, out):
    n = a.shape[0]
    out[:n] = a[...]
    out[n:] = b[...]


def join(run, a, b):
    n, d = a.shape
    return run(join_kernel, a, b, out_shape=shape((2 * n, d)), name="join")


def total_of(terms):
    total = 0.0
    for ref in terms:
        total = total + ref[...].astype(F32)
    return total


def sum_kernel(*refs):
    refs[-1][...] = total_of(refs[:-1])


def sum_of(run, terms):
    return run(sum_kernel, *terms, out_shape=shape(terms[0].shape, F32), name="sum")


def hidden_kernel(counts, *refs):
    sums, hidden = refs[-2:]
    h = sums.shape[1] // len(counts)
    at = 0
    for i, n in enumerate(counts):
        total = total_of(refs[at : at + n])
        at += n
        sums[:, i * h : (i + 1) * h, :] = total
        gate, up = total[0], total[1]
        hidden[0, i * h : (i + 1) * h, :] = (gate * jax.nn.sigmoid(gate) * up).astype(BF)


def hidden_of(run, groups):
    flat = [t for group in groups for t in group]
    _, h, half = flat[0].shape
    r = h * len(groups)
    return run(
        functools.partial(hidden_kernel, [len(g) for g in groups]),
        *flat,
        out_shape=[shape((2, r, half), F32), shape((1, r, half))],
        name="hidden",
    )


def grads_kernel(sums, *refs):
    terms, out = refs[:-1], refs[-1]
    total = 0.0
    for ref in terms:
        total = total + ref[0].astype(F32)
    gate, up = sums[0], sums[1]
    sig = jax.nn.sigmoid(gate)
    out[0] = (total * up * sig * (1.0 + gate * (1.0 - sig))).astype(BF)
    out[1] = (total * gate * sig).astype(BF)


def grads_of(run, sums, terms):
    _, r, half = sums.shape
    return run(
        grads_kernel,
        sums,
        *terms,
        out_shape=shape((2, r, half)),
        name="gate_up_grads",
    )


SLOTS = 4


def weight_kernel(which, expert, by_columns, swap, core, first, second, mine, other, *refs):
    token, slots, sem = refs[-3:]
    out = refs[-4]
    d = first.shape[1]
    half = mine.shape[2]
    db = slots.shape[1] if by_columns else slots.shape[2]
    token[...] = jnp.zeros(token.shape, F32)
    act = jnp.concatenate([first[...], second[...]], axis=0)
    if swap:
        act = swapped(act)
    base = core[0] * half
    bases = [pl.ds(pl.multiple_of(b, half), half) for b in (base, half - base)]
    pending = []

    def put(val, dst):
        i = len(pending)
        if i >= SLOTS:
            pending[i - SLOTS].wait()
        slots[i % SLOTS] = val
        copy = pltpu.make_async_copy(slots.at[i % SLOTS], dst, sem.at[i % SLOTS])
        copy.start()
        pending.append(copy)

    if by_columns:
        for j in range(d // db):
            cols = slice(j * db, (j + 1) * db)
            turned = act[:, cols].T
            for grads, part in zip((mine, other), bases):
                put(mm(turned, grads[which]), out.at[expert, pl.ds(j * db, db), part])
    else:
        for grads, part in zip((mine, other), bases):
            turned = grads[which].T
            for j in range(d // db):
                cols = slice(j * db, (j + 1) * db)
                put(mm(turned, act[:, cols]), out.at[expert, part, pl.ds(j * db, db)])
    for copy in pending[-SLOTS:]:
        copy.wait()


def weight_grads(run, core, first, second, mine, other, which, expert, experts, prev, by_columns, swap=False):
    h, d = first.shape
    _, r, half = mine.shape
    db = 512 if d % 512 == 0 else 128
    if by_columns:
        out = shape((experts, d, 2 * half), F32)
        slot = (SLOTS, db, half)
    else:
        out = shape((experts, 2 * half, d), F32)
        slot = (SLOTS, half, db)
    extra = [] if prev is None else [prev]
    return run(
        functools.partial(weight_kernel, which, expert, by_columns, swap),
        core,
        first,
        second,
        mine,
        other,
        *extra,
        in_specs=[SM] + [VM] * 4 + [AN] * len(extra),
        out_specs=[AN, VM],
        out_shape=[out, shape((8, 128), F32)],
        scratch=[pltpu.VMEM(slot, F32), pltpu.SemaphoreType.DMA((SLOTS,))],
        aliases={5: 0} if extra else {},
        name="weight_grad",
    )[0]


def combine_kernel(experts, weighted, *refs):
    pick, weight, keeps, gots = (refs[i * experts : (i + 1) * experts] for i in range(4))
    out, token, buf, sem = refs[-4:]
    token[...] = jnp.zeros(token.shape, F32)
    half = out.shape[1] // 2
    copies = []
    for i in range(2):
        cols = slice(i * half, (i + 1) * half)
        total = 0.0
        for e in range(experts):
            val = keeps[e][:, cols].astype(F32) + gots[e][:, cols].astype(F32)
            if weighted:
                val = weight[e][:, :1] * val
            total = total + lax.dot_general(
                pick[e][...], val.astype(BF), ROWS, preferred_element_type=F32
            )
        buf[i] = total.astype(BF)
        copies.append(
            pltpu.make_async_copy(buf.at[i], out.at[:, pl.ds(i * half, half)], sem.at[i])
        )
        copies[-1].start()
    for copy in copies:
        copy.wait()


def combine(run, pick, weight, pairs, weighted):
    experts, n = len(pick), pick[0].shape[1]
    d = pairs[0][0].shape[1]
    args = [*pick, *weight, *[p[0] for p in pairs], *[p[1] for p in pairs]]
    return run(
        functools.partial(combine_kernel, experts, weighted),
        *args,
        out_specs=[AN, VM],
        out_shape=[shape((n, d)), shape((8, 128), F32)],
        scratch=[pltpu.VMEM((2, n, d // 2), BF), pltpu.SemaphoreType.DMA((2,))],
        name="combine",
    )[0]


def build(n_dp, n_own):
    bits = n_dp.bit_length() - 1
    plain = list(range(bits - 1, -1, -1))
    mixed_order = plain[:-2] + [0, 1]

    def swap(x, bit):
        return lax.ppermute(x, "dp", [(i, i ^ (1 << bit)) for i in range(n_dp)])

    def swap_core(x):
        return lax.ppermute(x, "own", [(i, i ^ 1) for i in range(n_own)])

    def shift_x(x):
        return [
            lax.ppermute(x, "own", [(i, (i + 2 * k) % n_own) for i in range(n_own)])
            for k in range(1, n_own // 2)
        ]

    def gather(run, x, order):
        for bit in order[:-1]:
            got = swap(x, bit)
            yield None
            x = join(run, x, got)
        yield x, swap(x, order[-1])

    def scatter(run, keep, send, order):
        for bit in order[:0:-1]:
            got = swap(send, bit)
            yield None
            keep, send = halve(run, keep, got)
        yield keep, swap(send, order[0])

    def local(tokens, expert_ids, combine_weights, gate_weight, up_weight, down_weight, out_grad):
        run = Sequence()
        experts = gate_weight.shape[0]
        core = (lax.axis_index("own") % 2).astype(jnp.int32).reshape(1)
        ids, cw = expert_ids.T, combine_weights.T
        near = len(plain) - 1

        def steps(gen, n):
            for _ in range(n):
                res = next(gen)
            return res

        def up_gate_part(rows, e):
            keep, send = project(run, core, rows, [gate_weight, up_weight], e, False)
            return keep, swap_core(send)

        def grad_part(rows, e):
            keep, send = project(run, core, rows, [down_weight], e, True)
            return keep, swap_core(send)

        def across(part):
            return (*part, *shift_x(add(run, *part)))

        def hidden_pair(groups):
            sums, mine = hidden_of(run, groups)
            return sums, (mine, swap_core(mine))

        def grads_pair(sums, terms):
            mine = grads_of(run, sums, terms)
            return mine, swap_core(mine)

        def expert_out(hidden, e, mixed):
            pair = back(run, core, *hidden, [down_weight], e, False, mixed)
            gen = scatter(run, *pair, mixed_order if mixed else plain)
            next(gen)
            return gen

        def row_out(grads, e, mixed):
            pair = back(run, core, *grads, [gate_weight, up_weight], e, True, mixed)
            gen = scatter(run, *pair, mixed_order if mixed else plain)
            next(gen)
            return gen

        a0 = gather(run, rows_of(run, ids, tokens, 0), plain)
        next(a0)
        steps(a0, near - 1)
        a1 = gather(run, rows_of(run, ids, tokens, 1), plain)
        next(a1)
        rows0 = next(a0)
        p0a = up_gate_part(rows0[:1], 0)
        steps(a1, near - 1)
        s0, pick0, weight0 = scaled_of(run, ids, cw, out_grad, 0)
        g0 = gather(run, s0, plain)
        next(g0)
        u0a = across(p0a)
        rows1 = next(a1)
        steps(g0, near - 1)
        p0b = up_gate_part(rows0[1:], 0)
        s1, pick1, weight1 = scaled_of(run, ids, cw, out_grad, 1)
        g1 = gather(run, s1, plain)
        next(g1)
        u0b = across(p0b)
        u0a = (sum_of(run, u0a),)
        p1a = up_gate_part(rows1[:1], 1)
        scaled0 = next(g0)
        u1a = across(p1a)
        steps(g1, near - 1)
        p1b = up_gate_part(rows1[1:], 1)
        sums0, hidden0 = hidden_pair((u0a, u0b))
        u1b = across(p1b)
        scaled1 = next(g1)
        o0 = expert_out(hidden0, 0, False)
        u1a = (sum_of(run, u1a),)
        hp0 = grad_part(scaled0, 0)
        tick(run)
        h0 = across(hp0)
        sums1, hidden1 = hidden_pair((u1a, u1b))
        hp1 = grad_part(scaled1, 1)
        o1 = expert_out(hidden1, 1, True)
        h1 = across(hp1)
        pick, weight = (pick0, pick1), (weight0, weight1)
        d0 = grads_pair(sums0, h0)
        down = weight_grads(run, core, *scaled0, *hidden0, 0, 0, experts, None, False)
        q0 = row_out(d0, 0, False)
        next(o0)
        d1 = grads_pair(sums1, h1)
        down = weight_grads(run, core, *scaled1, *hidden1, 0, 1, experts, down, False)
        q1 = row_out(d1, 1, True)
        next(o1)
        gate = weight_grads(run, core, *rows0, *d0, 0, 0, experts, None, True)
        out0 = steps(o0, near - 1)
        next(q0)
        up = weight_grads(run, core, *rows0, *d0, 1, 0, experts, None, True)
        out1 = steps(o1, near - 1)
        next(q1)
        gate = weight_grads(run, core, *rows1, *d1, 0, 1, experts, gate, True)
        row0 = steps(q0, near - 1)
        mixed = combine(run, pick, weight, (out0, out1), True)
        row1 = steps(q1, near - 1)
        up = weight_grads(run, core, *rows1, *d1, 1, 1, experts, up, True)
        token_grad = combine(run, pick, weight, (row0, row1), False)
        return mixed, token_grad, gate, up, down

    return local


def solution(mesh):
    local = build(mesh.shape["dp"], mesh.shape["own"])
    in_specs = (
        P("dp", "own"),
        P("dp", None),
        P("dp", None),
        P(None, "own", "dp"),
        P(None, "own", "dp"),
        P(None, "dp", "own"),
        P("dp", "own"),
    )
    out_specs = (
        P("dp", "own"),
        P("dp", "own"),
        P(None, "own", "dp"),
        P(None, "own", "dp"),
        P(None, "dp", "own"),
    )
    return jax.shard_map(local, mesh=mesh, in_specs=in_specs, out_specs=out_specs, check_vma=False)
```

```python
import functools
import jax
import jax.numpy as jnp
from jax import lax
from jax.experimental import pallas as pl
from jax.experimental.pallas import tpu as pltpu
from jax.sharding import PartitionSpec as P

CAP = 40
BF = jnp.bfloat16
F32 = jnp.float32
MIB = 1024 * 1024
LIMIT = 16
VM = pl.BlockSpec(memory_space=pltpu.VMEM)
SM = pl.BlockSpec(memory_space=pltpu.SMEM)
AN = pl.BlockSpec(memory_space=pl.ANY)
ROWS = (((0,), (0,)), ((), ()))
LAST = (((1,), (1,)), ((), ()))


def shape(dims, dtype=BF):
    return jax.ShapeDtypeStruct(dims, dtype)


def mm(a, b):
    return jnp.dot(a, b, preferred_element_type=F32)


class Sequence:
    def __init__(self):
        self.last = None
        self.flops = 10**10

    def __call__(self, kernel, *args, out_shape, name, in_specs=None, out_specs=None, scratch=(), aliases=None):
        n_in = len(args)
        in_specs = list(in_specs or [VM] * n_in)
        args = list(args)
        extra = 0
        if self.last is not None:
            args.append(self.last)
            in_specs.append(AN)
            extra = 1

        def body(*refs):
            kernel(*refs[:n_in], *refs[n_in + extra :])

        if out_specs is None:
            out_specs = jax.tree.map(lambda o: VM, out_shape)
        out = pl.pallas_call(
            body,
            in_specs=in_specs,
            out_specs=out_specs,
            out_shape=out_shape,
            scratch_shapes=list(scratch),
            input_output_aliases=aliases or {},
            compiler_params=pltpu.CompilerParams(vmem_limit_bytes=LIMIT * MIB),
            cost_estimate=pl.CostEstimate(flops=self.flops, bytes_accessed=1, transcendentals=0),
            name=name,
        )(*args)
        self.last = min(jax.tree.leaves(out), key=lambda o: o.size)
        return out


def match_of(ids, expert):
    n = ids.shape[1]
    chosen = ids[...] == expert
    routed = jnp.sum(chosen.astype(F32), axis=0, keepdims=True)
    tri = (
        lax.broadcasted_iota(jnp.int32, (n, n), 0) <= lax.broadcasted_iota(jnp.int32, (n, n), 1)
    ).astype(BF)
    position = mm(jnp.broadcast_to(routed, (16, n)).astype(BF), tri)[:1].astype(jnp.int32) - 1
    slots = lax.broadcasted_iota(jnp.int32, (CAP, n), 0)
    match = (position == slots) & (routed > 0.0)
    return chosen, jnp.where(match, 1.0, 0.0)


def rows_kernel(expert, ids, tokens, out, held, sem):
    copy = pltpu.make_async_copy(tokens, held, sem)
    copy.start()
    _, match = match_of(ids, expert)
    copy.wait()
    out[...] = mm(match.astype(BF), held[...]).astype(BF)


def rows_of(run, ids, tokens, expert):
    return run(
        functools.partial(rows_kernel, expert),
        ids,
        pltpu.with_memory_space_constraint(tokens, pltpu.HBM),
        in_specs=[VM, AN],
        out_shape=shape((CAP, tokens.shape[1])),
        scratch=[pltpu.VMEM(tokens.shape, tokens.dtype), pltpu.SemaphoreType.DMA],
        name="rows",
    )


def scaled_kernel(expert, ids, cw, grad, scaled, pick, weight):
    chosen, match = match_of(ids, expert)
    w = jnp.sum(jnp.where(chosen, cw[...], 0.0), axis=0, keepdims=True)
    slot = jnp.sum(match * w, axis=1, keepdims=True)
    scaled[...] = (slot * mm(match.astype(BF), grad[...])).astype(BF)
    pick[...] = match.astype(BF)
    weight[...] = jnp.broadcast_to(slot, weight.shape)


def scaled_of(run, ids, cw, grad, expert):
    n, d = grad.shape
    return run(
        functools.partial(scaled_kernel, expert),
        ids,
        cw,
        grad,
        out_shape=[shape((CAP, d)), shape((CAP, n)), shape((CAP, 128), F32)],
        name="scaled",
    )


def tick_kernel(out):
    out[...] = jnp.zeros(out.shape, F32)


def tick(run):
    run(tick_kernel, out_shape=shape((8, 128), F32), name="tick")


def swapped(q):
    n = q.shape[0] // 4
    return jnp.concatenate([q[:n], q[2 * n : 3 * n], q[n : 2 * n], q[3 * n :]], axis=0)


def project_kernel(count, parts, expert, transposed, swap, core, *refs):
    acts, weights = refs[:count], refs[count : count + parts]
    outs = refs[count + parts :]
    act = acts[0][...] if count == 1 else jnp.concatenate([a[...] for a in acts], axis=0)
    if swap:
        act = swapped(act)
    half = outs[0].shape[2]
    fb = min(256, half)
    mine = core[0] * half
    for out, base in zip(outs, (mine, half - mine)):
        for p in range(parts):
            for j in range(half // fb):
                part = pl.ds(pl.multiple_of(base + j * fb, fb), fb)
                if transposed:
                    val = lax.dot_general(
                        act, weights[p][expert, part, :], LAST, preferred_element_type=F32
                    )
                else:
                    val = mm(act, weights[p][expert, :, part])
                out[p, :, j * fb : (j + 1) * fb] = val.astype(BF)


def project(run, core, acts, weights, expert, transposed, swap=False):
    h, d = acts[0].shape
    r = h * len(acts)
    f = weights[0].shape[1] if transposed else weights[0].shape[2]
    parts = len(weights)
    return run(
        functools.partial(project_kernel, len(acts), parts, expert, transposed, swap),
        core,
        *acts,
        *weights,
        in_specs=[SM] + [VM] * (len(acts) + parts),
        out_shape=[shape((parts, r, f // 2))] * 2,
        name="hidden_grad_part" if transposed else "gate_up_part",
    )


def back_kernel(parts, expert, transposed, swaps, core, mine, other, *refs):
    weights, outs = refs[:parts], refs[parts:]
    h, width = outs[0].shape
    d = width * len(swaps)
    half = mine.shape[2]
    db = 256 if d % 256 == 0 else 128
    first = core[0] * half
    bases = [pl.ds(pl.multiple_of(b, half), half) for b in (first, half - first)]
    for j in range(d // db):
        cols = slice(j * db, (j + 1) * db)
        total = None
        for p in range(parts):
            for act, base in zip((mine, other), bases):
                if transposed:
                    val = lax.dot_general(
                        act[p], weights[p][expert, cols, base], LAST, preferred_element_type=F32
                    )
                else:
                    val = mm(act[p], weights[p][expert, base, cols])
                total = val if total is None else total + val
        total = total.astype(BF)
        at = j * db // width
        if swaps[at]:
            total = swapped(total)
        cols = slice(j * db - at * width, (j + 1) * db - at * width)
        outs[2 * at][:, cols] = total[:h]
        outs[2 * at + 1][:, cols] = total[h:]


def back(run, core, mine, other, weights, expert, transposed, swaps):
    parts, r, _ = mine.shape
    d = weights[0].shape[1] if transposed else weights[0].shape[2]
    return run(
        functools.partial(back_kernel, parts, expert, transposed, swaps),
        core,
        mine,
        other,
        *weights,
        in_specs=[SM] + [VM] * (2 + parts),
        out_shape=[shape((r // 2, d // len(swaps)))] * (2 * len(swaps)),
        name="row_grad_part" if transposed else "expert_part",
    )


def add_kernel(keep, got, out):
    out[...] = (keep[...].astype(F32) + got[...].astype(F32)).astype(BF)


def add(run, keep, got):
    return run(
        add_kernel,
        keep,
        got,
        out_shape=shape(keep.shape),
        name="add",
    )


def halve_kernel(keep, got, out_keep, out_send):
    h = out_keep.shape[0]
    total = (keep[...].astype(F32) + got[...].astype(F32)).astype(BF)
    out_keep[...] = total[:h]
    out_send[...] = total[h:]


def halve(run, keep, got):
    r, d = keep.shape
    return run(
        halve_kernel,
        keep,
        got,
        out_shape=[shape((r // 2, d))] * 2,
        name="halve",
    )


def join_kernel(a, b, out):
    n = a.shape[0]
    out[:n] = a[...]
    out[n:] = b[...]


def join(run, a, b):
    n, d = a.shape
    return run(join_kernel, a, b, out_shape=shape((2 * n, d)), name="join")


def total_of(terms):
    total = 0.0
    for ref in terms:
        total = total + ref[...].astype(F32)
    return total


def sum_kernel(*refs):
    refs[-1][...] = total_of(refs[:-1])


def sum_of(run, terms):
    return run(sum_kernel, *terms, out_shape=shape(terms[0].shape, F32), name="sum")


def hidden_kernel(counts, *refs):
    sums, hidden = refs[-2:]
    h = sums.shape[1] // len(counts)
    at = 0
    for i, n in enumerate(counts):
        total = total_of(refs[at : at + n])
        at += n
        sums[:, i * h : (i + 1) * h, :] = total
        gate, up = total[0], total[1]
        hidden[0, i * h : (i + 1) * h, :] = (gate * jax.nn.sigmoid(gate) * up).astype(BF)


def hidden_of(run, groups):
    flat = [t for group in groups for t in group]
    _, h, half = flat[0].shape
    r = h * len(groups)
    return run(
        functools.partial(hidden_kernel, [len(g) for g in groups]),
        *flat,
        out_shape=[shape((2, r, half), F32), shape((1, r, half))],
        name="hidden",
    )


def grads_kernel(sums, *refs):
    terms, out = refs[:-1], refs[-1]
    total = 0.0
    for ref in terms:
        total = total + ref[0].astype(F32)
    gate, up = sums[0], sums[1]
    sig = jax.nn.sigmoid(gate)
    out[0] = (total * up * sig * (1.0 + gate * (1.0 - sig))).astype(BF)
    out[1] = (total * gate * sig).astype(BF)


def grads_of(run, sums, terms):
    _, r, half = sums.shape
    return run(
        grads_kernel,
        sums,
        *terms,
        out_shape=shape((2, r, half)),
        name="gate_up_grads",
    )


SLOTS = 4


def weight_kernel(which, expert, by_columns, swap, core, first, second, mine, other, *refs):
    token, slots, sem = refs[-3:]
    out = refs[-4]
    d = first.shape[1]
    half = mine.shape[2]
    db = slots.shape[1] if by_columns else slots.shape[2]
    token[...] = jnp.zeros(token.shape, F32)
    act = jnp.concatenate([first[...], second[...]], axis=0)
    if swap:
        act = swapped(act)
    base = core[0] * half
    bases = [pl.ds(pl.multiple_of(b, half), half) for b in (base, half - base)]
    pending = []

    def put(val, dst):
        i = len(pending)
        if i >= SLOTS:
            pending[i - SLOTS].wait()
        slots[i % SLOTS] = val
        copy = pltpu.make_async_copy(slots.at[i % SLOTS], dst, sem.at[i % SLOTS])
        copy.start()
        pending.append(copy)

    if by_columns:
        for j in range(d // db):
            cols = slice(j * db, (j + 1) * db)
            turned = act[:, cols].T
            for grads, part in zip((mine, other), bases):
                put(mm(turned, grads[which]), out.at[expert, pl.ds(j * db, db), part])
    else:
        for grads, part in zip((mine, other), bases):
            turned = grads[which].T
            for j in range(d // db):
                cols = slice(j * db, (j + 1) * db)
                put(mm(turned, act[:, cols]), out.at[expert, part, pl.ds(j * db, db)])
    for copy in pending[-SLOTS:]:
        copy.wait()


def weight_grads(run, core, first, second, mine, other, which, expert, experts, prev, by_columns, swap=False):
    h, d = first.shape
    _, r, half = mine.shape
    db = 512 if d % 512 == 0 else 128
    if by_columns:
        out = shape((experts, d, 2 * half), F32)
        slot = (SLOTS, db, half)
    else:
        out = shape((experts, 2 * half, d), F32)
        slot = (SLOTS, half, db)
    extra = [] if prev is None else [prev]
    return run(
        functools.partial(weight_kernel, which, expert, by_columns, swap),
        core,
        first,
        second,
        mine,
        other,
        *extra,
        in_specs=[SM] + [VM] * 4 + [AN] * len(extra),
        out_specs=[AN, VM],
        out_shape=[out, shape((8, 128), F32)],
        scratch=[pltpu.VMEM(slot, F32), pltpu.SemaphoreType.DMA((SLOTS,))],
        aliases={5: 0} if extra else {},
        name="weight_grad",
    )[0]


def combine_kernel(experts, weighted, *refs):
    pick, weight, keeps, gots = (refs[i * experts : (i + 1) * experts] for i in range(4))
    out, token, buf, sem = refs[-4:]
    token[...] = jnp.zeros(token.shape, F32)
    half = out.shape[1] // 2
    copies = []
    for i in range(2):
        cols = slice(i * half, (i + 1) * half)
        total = 0.0
        for e in range(experts):
            val = keeps[e][:, cols].astype(F32) + gots[e][:, cols].astype(F32)
            if weighted:
                val = weight[e][:, :1] * val
            total = total + lax.dot_general(
                pick[e][...], val.astype(BF), ROWS, preferred_element_type=F32
            )
        buf[i] = total.astype(BF)
        copies.append(
            pltpu.make_async_copy(buf.at[i], out.at[:, pl.ds(i * half, half)], sem.at[i])
        )
        copies[-1].start()
    for copy in copies:
        copy.wait()


def combine(run, pick, weight, pairs, weighted):
    experts, n = len(pick), pick[0].shape[1]
    d = pairs[0][0].shape[1]
    args = [*pick, *weight, *[p[0] for p in pairs], *[p[1] for p in pairs]]
    return run(
        functools.partial(combine_kernel, experts, weighted),
        *args,
        out_specs=[AN, VM],
        out_shape=[shape((n, d)), shape((8, 128), F32)],
        scratch=[pltpu.VMEM((2, n, d // 2), BF), pltpu.SemaphoreType.DMA((2,))],
        name="combine",
    )[0]


def build(n_dp, n_own):
    bits = n_dp.bit_length() - 1
    plain = list(range(bits - 1, -1, -1))
    mixed_order = plain[:-2] + [0, 1]

    def swap(x, bit):
        return lax.ppermute(x, "dp", [(i, i ^ (1 << bit)) for i in range(n_dp)])

    def swap_core(x):
        return lax.ppermute(x, "own", [(i, i ^ 1) for i in range(n_own)])

    def shift_x(x):
        return [
            lax.ppermute(x, "own", [(i, (i + 2 * k) % n_own) for i in range(n_own)])
            for k in range(1, n_own // 2)
        ]

    def gather(run, x, order):
        for bit in order[:-1]:
            got = swap(x, bit)
            yield None
            x = join(run, x, got)
        yield x, swap(x, order[-1])

    def scatter(run, keep, send, order):
        for bit in order[:0:-1]:
            got = swap(send, bit)
            yield None
            keep, send = halve(run, keep, got)
        yield keep, swap(send, order[0])

    def local(tokens, expert_ids, combine_weights, gate_weight, up_weight, down_weight, out_grad):
        run = Sequence()
        experts = gate_weight.shape[0]
        core = (lax.axis_index("own") % 2).astype(jnp.int32).reshape(1)
        ids, cw = expert_ids.T, combine_weights.T
        near = len(plain) - 1

        def steps(gen, n):
            for _ in range(n):
                res = next(gen)
            return res

        def up_gate_part(rows, e):
            keep, send = project(run, core, rows, [gate_weight, up_weight], e, False)
            return keep, swap_core(send)

        def grad_part(rows, e):
            keep, send = project(run, core, rows, [down_weight], e, True)
            return keep, swap_core(send)

        def across(part):
            return (*part, *shift_x(add(run, *part)))

        def hidden_pair(groups):
            sums, mine = hidden_of(run, groups)
            return sums, (mine, swap_core(mine))

        def grads_pair(sums, terms):
            mine = grads_of(run, sums, terms)
            return mine, swap_core(mine)

        def expert_out(hidden, e, mixed):
            pair = back(run, core, *hidden, [down_weight], e, False, (mixed,))
            gen = scatter(run, *pair, mixed_order if mixed else plain)
            next(gen)
            return gen

        def row_out(grads, e, mixed):
            pair = back(run, core, *grads, [gate_weight, up_weight], e, True, (mixed,))
            gen = scatter(run, *pair, mixed_order if mixed else plain)
            next(gen)
            return gen

        a0 = gather(run, rows_of(run, ids, tokens, 0), plain)
        next(a0)
        steps(a0, near - 1)
        a1 = gather(run, rows_of(run, ids, tokens, 1), plain)
        next(a1)
        rows0 = next(a0)
        p0a = up_gate_part(rows0[:1], 0)
        steps(a1, near - 1)
        s0, pick0, weight0 = scaled_of(run, ids, cw, out_grad, 0)
        g0 = gather(run, s0, plain)
        next(g0)
        u0a = across(p0a)
        rows1 = next(a1)
        steps(g0, near - 1)
        p0b = up_gate_part(rows0[1:], 0)
        s1, pick1, weight1 = scaled_of(run, ids, cw, out_grad, 1)
        g1 = gather(run, s1, plain)
        next(g1)
        u0b = across(p0b)
        u0a = (sum_of(run, u0a),)
        p1a = up_gate_part(rows1[:1], 1)
        scaled0 = next(g0)
        u1a = across(p1a)
        steps(g1, near - 1)
        p1b = up_gate_part(rows1[1:], 1)
        sums0, hidden0 = hidden_pair((u0a, u0b))
        u1b = across(p1b)
        scaled1 = next(g1)
        o0 = expert_out(hidden0, 0, False)
        u1a = (sum_of(run, u1a),)
        hp0 = grad_part(scaled0, 0)
        tick(run)
        h0 = across(hp0)
        sums1, hidden1 = hidden_pair((u1a, u1b))
        hp1 = grad_part(scaled1, 1)
        o1 = expert_out(hidden1, 1, True)
        h1 = across(hp1)
        d0 = grads_pair(sums0, h0)
        down = weight_grads(run, core, *scaled0, *hidden0, 0, 0, experts, None, False)
        q0 = row_out(d0, 0, False)
        next(o0)
        d1 = grads_pair(sums1, h1)
        down = weight_grads(run, core, *scaled1, *hidden1, 0, 1, experts, down, False)
        q1 = row_out(d1, 1, True)
        next(o1)
        gate = weight_grads(run, core, *rows0, *d0, 0, 0, experts, None, True)
        out0 = steps(o0, near - 1)
        next(q0)
        up = weight_grads(run, core, *rows0, *d0, 1, 0, experts, None, True)
        out1 = steps(o1, near - 1)
        next(q1)
        gate = weight_grads(run, core, *rows1, *d1, 0, 1, experts, gate, True)
        row0 = steps(q0, near - 1)
        row1 = steps(q1, near - 1)
        up = weight_grads(run, core, *rows1, *d1, 1, 1, experts, up, True)
        mixed = combine(run, (pick0, pick1), (weight0, weight1), (out0, out1), True)
        token_grad = combine(run, (pick0, pick1), (weight0, weight1), (row0, row1), False)
        return mixed, token_grad, gate, up, down

    return local


def solution(mesh):
    local = build(mesh.shape["dp"], mesh.shape["own"])
    in_specs = (
        P("dp", "own"),
        P("dp", None),
        P("dp", None),
        P(None, "own", "dp"),
        P(None, "own", "dp"),
        P(None, "dp", "own"),
        P("dp", "own"),
    )
    out_specs = (
        P("dp", "own"),
        P("dp", "own"),
        P(None, "own", "dp"),
        P(None, "own", "dp"),
        P(None, "dp", "own"),
    )
    return jax.shard_map(local, mesh=mesh, in_specs=in_specs, out_specs=out_specs, check_vma=False)
```

```python
import functools
import jax
import jax.numpy as jnp
from jax import lax
from jax.experimental import pallas as pl
from jax.experimental.pallas import tpu as pltpu
from jax.sharding import PartitionSpec as P

CAP = 40
BF = jnp.bfloat16
F32 = jnp.float32
MIB = 1024 * 1024
LIMIT = 16
VM = pl.BlockSpec(memory_space=pltpu.VMEM)
SM = pl.BlockSpec(memory_space=pltpu.SMEM)
AN = pl.BlockSpec(memory_space=pl.ANY)
ROWS = (((0,), (0,)), ((), ()))
LAST = (((1,), (1,)), ((), ()))


def shape(dims, dtype=BF):
    return jax.ShapeDtypeStruct(dims, dtype)


def mm(a, b):
    return jnp.dot(a, b, preferred_element_type=F32)


class Sequence:
    def __init__(self):
        self.last = None
        self.flops = 10**10

    def __call__(self, kernel, *args, out_shape, name, in_specs=None, out_specs=None, scratch=(), aliases=None):
        n_in = len(args)
        in_specs = list(in_specs or [VM] * n_in)
        args = list(args)
        extra = 0
        if self.last is not None:
            args.append(self.last)
            in_specs.append(AN)
            extra = 1

        def body(*refs):
            kernel(*refs[:n_in], *refs[n_in + extra :])

        if out_specs is None:
            out_specs = jax.tree.map(lambda o: VM, out_shape)
        out = pl.pallas_call(
            body,
            in_specs=in_specs,
            out_specs=out_specs,
            out_shape=out_shape,
            scratch_shapes=list(scratch),
            input_output_aliases=aliases or {},
            compiler_params=pltpu.CompilerParams(vmem_limit_bytes=LIMIT * MIB),
            cost_estimate=pl.CostEstimate(flops=self.flops, bytes_accessed=1, transcendentals=0),
            name=name,
        )(*args)
        self.last = min(jax.tree.leaves(out), key=lambda o: o.size)
        return out


def match_of(ids, expert):
    n = ids.shape[1]
    chosen = ids[...] == expert
    routed = jnp.sum(chosen.astype(F32), axis=0, keepdims=True)
    tri = (
        lax.broadcasted_iota(jnp.int32, (n, n), 0) <= lax.broadcasted_iota(jnp.int32, (n, n), 1)
    ).astype(BF)
    position = mm(jnp.broadcast_to(routed, (16, n)).astype(BF), tri)[:1].astype(jnp.int32) - 1
    slots = lax.broadcasted_iota(jnp.int32, (CAP, n), 0)
    match = (position == slots) & (routed > 0.0)
    return chosen, jnp.where(match, 1.0, 0.0)


def rows_kernel(expert, ids, tokens, out, held, sem):
    copy = pltpu.make_async_copy(tokens, held, sem)
    copy.start()
    _, match = match_of(ids, expert)
    copy.wait()
    out[...] = mm(match.astype(BF), held[...]).astype(BF)


def rows_of(run, ids, tokens, expert):
    return run(
        functools.partial(rows_kernel, expert),
        ids,
        pltpu.with_memory_space_constraint(tokens, pltpu.HBM),
        in_specs=[VM, AN],
        out_shape=shape((CAP, tokens.shape[1])),
        scratch=[pltpu.VMEM(tokens.shape, tokens.dtype), pltpu.SemaphoreType.DMA],
        name="rows",
    )


def scaled_kernel(expert, ids, cw, grad, scaled, pick, weight):
    chosen, match = match_of(ids, expert)
    w = jnp.sum(jnp.where(chosen, cw[...], 0.0), axis=0, keepdims=True)
    slot = jnp.sum(match * w, axis=1, keepdims=True)
    scaled[...] = (slot * mm(match.astype(BF), grad[...])).astype(BF)
    pick[...] = match.astype(BF)
    weight[...] = jnp.broadcast_to(slot, weight.shape)


def scaled_of(run, ids, cw, grad, expert):
    n, d = grad.shape
    return run(
        functools.partial(scaled_kernel, expert),
        ids,
        cw,
        grad,
        out_shape=[shape((CAP, d)), shape((CAP, n)), shape((CAP, 128), F32)],
        name="scaled",
    )


def tick_kernel(out):
    out[...] = jnp.zeros(out.shape, F32)


def tick(run):
    run(tick_kernel, out_shape=shape((8, 128), F32), name="tick")


def swapped(q):
    n = q.shape[0] // 4
    return jnp.concatenate([q[:n], q[2 * n : 3 * n], q[n : 2 * n], q[3 * n :]], axis=0)


def project_kernel(count, parts, expert, transposed, swap, core, *refs):
    acts, weights = refs[:count], refs[count : count + parts]
    outs = refs[count + parts :]
    act = acts[0][...] if count == 1 else jnp.concatenate([a[...] for a in acts], axis=0)
    if swap:
        act = swapped(act)
    half = outs[0].shape[2]
    fb = min(256, half)
    mine = core[0] * half
    for out, base in zip(outs, (mine, half - mine)):
        for p in range(parts):
            for j in range(half // fb):
                part = pl.ds(pl.multiple_of(base + j * fb, fb), fb)
                if transposed:
                    val = lax.dot_general(
                        act, weights[p][expert, part, :], LAST, preferred_element_type=F32
                    )
                else:
                    val = mm(act, weights[p][expert, :, part])
                out[p, :, j * fb : (j + 1) * fb] = val.astype(BF)


def project(run, core, acts, weights, expert, transposed, swap=False):
    h, d = acts[0].shape
    r = h * len(acts)
    f = weights[0].shape[1] if transposed else weights[0].shape[2]
    parts = len(weights)
    return run(
        functools.partial(project_kernel, len(acts), parts, expert, transposed, swap),
        core,
        *acts,
        *weights,
        in_specs=[SM] + [VM] * (len(acts) + parts),
        out_shape=[shape((parts, r, f // 2))] * 2,
        name="hidden_grad_part" if transposed else "gate_up_part",
    )


def back_kernel(parts, expert, transposed, swaps, core, mine, other, *refs):
    weights, outs = refs[:parts], refs[parts:]
    h, width = outs[0].shape
    d = width * len(swaps)
    half = mine.shape[2]
    db = 256 if d % 256 == 0 else 128
    first = core[0] * half
    bases = [pl.ds(pl.multiple_of(b, half), half) for b in (first, half - first)]
    for j in range(d // db):
        cols = slice(j * db, (j + 1) * db)
        total = None
        for p in range(parts):
            for act, base in zip((mine, other), bases):
                if transposed:
                    val = lax.dot_general(
                        act[p], weights[p][expert, cols, base], LAST, preferred_element_type=F32
                    )
                else:
                    val = mm(act[p], weights[p][expert, base, cols])
                total = val if total is None else total + val
        total = total.astype(BF)
        at = j * db // width
        if swaps[at]:
            total = swapped(total)
        cols = slice(j * db - at * width, (j + 1) * db - at * width)
        outs[2 * at][:, cols] = total[:h]
        outs[2 * at + 1][:, cols] = total[h:]


def back(run, core, mine, other, weights, expert, transposed, swaps):
    parts, r, _ = mine.shape
    d = weights[0].shape[1] if transposed else weights[0].shape[2]
    return run(
        functools.partial(back_kernel, parts, expert, transposed, swaps),
        core,
        mine,
        other,
        *weights,
        in_specs=[SM] + [VM] * (2 + parts),
        out_shape=[shape((r // 2, d // len(swaps)))] * (2 * len(swaps)),
        name="row_grad_part" if transposed else "expert_part",
    )


def add_kernel(keep, got, out):
    out[...] = (keep[...].astype(F32) + got[...].astype(F32)).astype(BF)


def add(run, keep, got):
    return run(
        add_kernel,
        keep,
        got,
        out_shape=shape(keep.shape),
        name="add",
    )


def halve_kernel(keep, got, out_keep, out_send):
    h = out_keep.shape[0]
    total = (keep[...].astype(F32) + got[...].astype(F32)).astype(BF)
    out_keep[...] = total[:h]
    out_send[...] = total[h:]


def halve(run, keep, got):
    r, d = keep.shape
    return run(
        halve_kernel,
        keep,
        got,
        out_shape=[shape((r // 2, d))] * 2,
        name="halve",
    )


def join_kernel(a, b, out):
    n = a.shape[0]
    out[:n] = a[...]
    out[n:] = b[...]


def join(run, a, b):
    n, d = a.shape
    return run(join_kernel, a, b, out_shape=shape((2 * n, d)), name="join")


def total_of(terms):
    total = 0.0
    for ref in terms:
        total = total + ref[...].astype(F32)
    return total


def sum_kernel(*refs):
    refs[-1][...] = total_of(refs[:-1])


def sum_of(run, terms):
    return run(sum_kernel, *terms, out_shape=shape(terms[0].shape, F32), name="sum")


def hidden_kernel(counts, *refs):
    sums, hidden = refs[-2:]
    h = sums.shape[1] // len(counts)
    at = 0
    for i, n in enumerate(counts):
        total = total_of(refs[at : at + n])
        at += n
        sums[:, i * h : (i + 1) * h, :] = total
        gate, up = total[0], total[1]
        hidden[0, i * h : (i + 1) * h, :] = (gate * jax.nn.sigmoid(gate) * up).astype(BF)


def hidden_of(run, groups):
    flat = [t for group in groups for t in group]
    _, h, half = flat[0].shape
    r = h * len(groups)
    return run(
        functools.partial(hidden_kernel, [len(g) for g in groups]),
        *flat,
        out_shape=[shape((2, r, half), F32), shape((1, r, half))],
        name="hidden",
    )


def grads_kernel(sums, *refs):
    terms, out = refs[:-1], refs[-1]
    total = 0.0
    for ref in terms:
        total = total + ref[0].astype(F32)
    gate, up = sums[0], sums[1]
    sig = jax.nn.sigmoid(gate)
    out[0] = (total * up * sig * (1.0 + gate * (1.0 - sig))).astype(BF)
    out[1] = (total * gate * sig).astype(BF)


def grads_of(run, sums, terms):
    _, r, half = sums.shape
    return run(
        grads_kernel,
        sums,
        *terms,
        out_shape=shape((2, r, half)),
        name="gate_up_grads",
    )


SLOTS = 4


def weight_kernel(which, expert, by_columns, swap, core, first, second, mine, other, *refs):
    token, slots, sem = refs[-3:]
    out = refs[-4]
    d = first.shape[1]
    half = mine.shape[2]
    db = slots.shape[1] if by_columns else slots.shape[2]
    token[...] = jnp.zeros(token.shape, F32)
    act = jnp.concatenate([first[...], second[...]], axis=0)
    if swap:
        act = swapped(act)
    base = core[0] * half
    bases = [pl.ds(pl.multiple_of(b, half), half) for b in (base, half - base)]
    pending = []

    def put(val, dst):
        i = len(pending)
        if i >= SLOTS:
            pending[i - SLOTS].wait()
        slots[i % SLOTS] = val
        copy = pltpu.make_async_copy(slots.at[i % SLOTS], dst, sem.at[i % SLOTS])
        copy.start()
        pending.append(copy)

    if by_columns:
        for j in range(d // db):
            cols = slice(j * db, (j + 1) * db)
            turned = act[:, cols].T
            for grads, part in zip((mine, other), bases):
                put(mm(turned, grads[which]), out.at[expert, pl.ds(j * db, db), part])
    else:
        for grads, part in zip((mine, other), bases):
            turned = grads[which].T
            for j in range(d // db):
                cols = slice(j * db, (j + 1) * db)
                put(mm(turned, act[:, cols]), out.at[expert, part, pl.ds(j * db, db)])
    for copy in pending[-SLOTS:]:
        copy.wait()


def weight_grads(run, core, first, second, mine, other, which, expert, experts, prev, by_columns, swap=False):
    h, d = first.shape
    _, r, half = mine.shape
    db = 512 if d % 512 == 0 else 128
    if by_columns:
        out = shape((experts, d, 2 * half), F32)
        slot = (SLOTS, db, half)
    else:
        out = shape((experts, 2 * half, d), F32)
        slot = (SLOTS, half, db)
    extra = [] if prev is None else [prev]
    return run(
        functools.partial(weight_kernel, which, expert, by_columns, swap),
        core,
        first,
        second,
        mine,
        other,
        *extra,
        in_specs=[SM] + [VM] * 4 + [AN] * len(extra),
        out_specs=[AN, VM],
        out_shape=[out, shape((8, 128), F32)],
        scratch=[pltpu.VMEM(slot, F32), pltpu.SemaphoreType.DMA((SLOTS,))],
        aliases={5: 0} if extra else {},
        name="weight_grad",
    )[0]


def combine_kernel(experts, weighted, *refs):
    pick, weight, keeps, gots = (refs[i * experts : (i + 1) * experts] for i in range(4))
    out, token, buf, sem = refs[-4:]
    token[...] = jnp.zeros(token.shape, F32)
    half = out.shape[1] // 2
    copies = []
    for i in range(2):
        cols = slice(i * half, (i + 1) * half)
        total = 0.0
        for e in range(experts):
            val = keeps[e][:, cols].astype(F32) + gots[e][:, cols].astype(F32)
            if weighted:
                val = weight[e][:, :1] * val
            total = total + lax.dot_general(
                pick[e][...], val.astype(BF), ROWS, preferred_element_type=F32
            )
        buf[i] = total.astype(BF)
        copies.append(
            pltpu.make_async_copy(buf.at[i], out.at[:, pl.ds(i * half, half)], sem.at[i])
        )
        copies[-1].start()
    for copy in copies:
        copy.wait()


def combine(run, pick, weight, pairs, weighted):
    experts, n = len(pick), pick[0].shape[1]
    d = pairs[0][0].shape[1]
    args = [*pick, *weight, *[p[0] for p in pairs], *[p[1] for p in pairs]]
    return run(
        functools.partial(combine_kernel, experts, weighted),
        *args,
        out_specs=[AN, VM],
        out_shape=[shape((n, d)), shape((8, 128), F32)],
        scratch=[pltpu.VMEM((2, n, d // 2), BF), pltpu.SemaphoreType.DMA((2,))],
        name="combine",
    )[0]


def build(n_dp, n_own):
    bits = n_dp.bit_length() - 1
    plain = list(range(bits - 1, -1, -1))
    mixed_order = plain[:-2] + [0, 1]

    def swap(x, bit):
        return lax.ppermute(x, "dp", [(i, i ^ (1 << bit)) for i in range(n_dp)])

    def swap_core(x):
        return lax.ppermute(x, "own", [(i, i ^ 1) for i in range(n_own)])

    def shift_x(x):
        return [
            lax.ppermute(x, "own", [(i, (i + 2 * k) % n_own) for i in range(n_own)])
            for k in range(1, n_own // 2)
        ]

    def gather(run, x, order):
        for bit in order[:-1]:
            got = swap(x, bit)
            yield None
            x = join(run, x, got)
        yield x, swap(x, order[-1])

    def scatter(run, keep, send, order):
        for bit in order[:0:-1]:
            got = swap(send, bit)
            yield None
            keep, send = halve(run, keep, got)
        yield keep, swap(send, order[0])

    def local(tokens, expert_ids, combine_weights, gate_weight, up_weight, down_weight, out_grad):
        run = Sequence()
        experts = gate_weight.shape[0]
        core = (lax.axis_index("own") % 2).astype(jnp.int32).reshape(1)
        ids, cw = expert_ids.T, combine_weights.T
        near = len(plain) - 1

        def steps(gen, n):
            for _ in range(n):
                res = next(gen)
            return res

        def up_gate_part(rows, e):
            keep, send = project(run, core, rows, [gate_weight, up_weight], e, False)
            return keep, swap_core(send)

        def grad_part(rows, e):
            keep, send = project(run, core, rows, [down_weight], e, True)
            return keep, swap_core(send)

        def across(part):
            return (*part, *shift_x(add(run, *part)))

        def hidden_pair(groups):
            sums, mine = hidden_of(run, groups)
            return sums, (mine, swap_core(mine))

        def grads_pair(sums, terms):
            mine = grads_of(run, sums, terms)
            return mine, swap_core(mine)

        def expert_out(hidden, e, mixed):
            pair = back(run, core, *hidden, [down_weight], e, False, (mixed,))
            gen = scatter(run, *pair, mixed_order if mixed else plain)
            next(gen)
            return gen

        def row_out(grads, e, mixed):
            pair = back(run, core, *grads, [gate_weight, up_weight], e, True, (mixed,))
            gen = scatter(run, *pair, mixed_order if mixed else plain)
            next(gen)
            return gen

        a0 = gather(run, rows_of(run, ids, tokens, 0), plain)
        next(a0)
        steps(a0, near - 1)
        a1 = gather(run, rows_of(run, ids, tokens, 1), plain)
        next(a1)
        rows0 = next(a0)
        p0a = up_gate_part(rows0[:1], 0)
        steps(a1, near - 1)
        s0, pick0, weight0 = scaled_of(run, ids, cw, out_grad, 0)
        g0 = gather(run, s0, plain)
        next(g0)
        u0a = across(p0a)
        rows1 = next(a1)
        steps(g0, near - 1)
        p0b = up_gate_part(rows0[1:], 0)
        s1, pick1, weight1 = scaled_of(run, ids, cw, out_grad, 1)
        g1 = gather(run, s1, plain)
        next(g1)
        u0b = across(p0b)
        u0a = (sum_of(run, u0a),)
        p1a = up_gate_part(rows1[:1], 1)
        scaled0 = next(g0)
        u1a = across(p1a)
        steps(g1, near - 1)
        p1b = up_gate_part(rows1[1:], 1)
        sums0, hidden0 = hidden_pair((u0a, u0b))
        u1b = across(p1b)
        scaled1 = next(g1)
        o0 = expert_out(hidden0, 0, False)
        u1a = (sum_of(run, u1a),)
        hp0 = grad_part(scaled0, 0)
        tick(run)
        h0 = across(hp0)
        sums1, hidden1 = hidden_pair((u1a, u1b))
        hp1 = grad_part(scaled1, 1)
        o1 = expert_out(hidden1, 1, True)
        h1 = across(hp1)
        d0 = grads_pair(sums0, h0)
        down = weight_grads(run, core, *scaled0, *hidden0, 0, 0, experts, None, False)
        q0 = row_out(d0, 0, False)
        next(o0)
        d1 = grads_pair(sums1, h1)
        down = weight_grads(run, core, *scaled1, *hidden1, 0, 1, experts, down, False)
        q1 = row_out(d1, 1, True)
        next(o1)
        gate = weight_grads(run, core, *rows0, *d0, 0, 0, experts, None, True)
        next(q0)
        up = weight_grads(run, core, *rows0, *d0, 1, 0, experts, None, True)
        next(q1)
        out0 = steps(o0, near - 1)
        out1 = steps(o1, near - 1)
        gate = weight_grads(run, core, *rows1, *d1, 0, 1, experts, gate, True)
        row0 = steps(q0, near - 1)
        row1 = steps(q1, near - 1)
        up = weight_grads(run, core, *rows1, *d1, 1, 1, experts, up, True)
        mixed = combine(run, (pick0, pick1), (weight0, weight1), (out0, out1), True)
        token_grad = combine(run, (pick0, pick1), (weight0, weight1), (row0, row1), False)
        return mixed, token_grad, gate, up, down

    return local


def solution(mesh):
    local = build(mesh.shape["dp"], mesh.shape["own"])
    in_specs = (
        P("dp", "own"),
        P("dp", None),
        P("dp", None),
        P(None, "own", "dp"),
        P(None, "own", "dp"),
        P(None, "dp", "own"),
        P("dp", "own"),
    )
    out_specs = (
        P("dp", "own"),
        P("dp", "own"),
        P(None, "own", "dp"),
        P(None, "own", "dp"),
        P(None, "dp", "own"),
    )
    return jax.shard_map(local, mesh=mesh, in_specs=in_specs, out_specs=out_specs, check_vma=False)
```
